32 devices in a mesh: groups: 2 (over y), tp: 4 (over z), dp: 4 (over x, core).
Axes of the slice: x: 2, y: 2, z: 4, core: 2. Of those that a mesh axis runs over, the one named last changes fastest.
Arguments:
- tokens: bfloat16 [4, 32, 8192], P(None, ('groups', 'dp'), 'tp'), parts along dimension 1, may hold values from -6 to 6
- lengths: int32 [32], P(('groups', 'dp')), parts along dimension 0, may hold values from 1 to 192, as said below
- cache_keys: bfloat16 [32, 192, 1024], P(('groups', 'dp'), 'tp'), parts along dimension 0, may hold values from -64 to 64
- cache_values: bfloat16 [32, 192, 1024], P(('groups', 'dp'), 'tp'), parts along dimension 0, may hold values from -6 to 6
- q_weight: bfloat16 [8192, 8192], P('dp', 'tp'), may hold values from -0.0625 to 0.0625
- kv_weight: bfloat16 [8192, 2048], P('tp'), may hold values from -0.0625 to 0.0625
- o_weight: bfloat16 [8192, 8192], P('tp', 'dp'), may hold values from -0.0625 to 0.0625
- adapters: bfloat16 [4, 64, 8192], P(None, None, ('tp', 'dp')), may hold values from -0.1875 to 0.1875
- layout: int32 [16], replicated, may hold values from 0 to 15, each once
Outputs:
- mixed: bfloat16 [4, 32, 8192], P(None, ('groups', 'dp'), 'tp'), parts along dimension 1
The draws below stay inside these ranges and needn't reach their ends.
There are 2 independent parts, one for each index of `groups`. The reference program is written for one: setup_inputs(seed, part) draws one part's arguments, and reference() takes and returns one part's arrays. A program takes and returns all parts, laid end to end along the dimension named above; an argument that names none is the same for every part. Nothing has to cross between parts.
Inputs may be any that keep to these rules, and one draw needn't show every extreme that they name: `lengths`: one sequence has exactly 192 cached positions.
All inputs are finite; a program needn't handle non-finite values.
Results may differ from the reference program's by a relative error of at most 0.008.
The reference program's roundings to bfloat16 on the way (of `ordered`, `q_merged`, `o_merged`, `queries`, `new_kv` and `attn`) count: a program that leaves them out, or rounds other values in their place, can miss the bound.
Values may be sent and summed in bfloat16 or wider, within the bound.
No kernel may reach another device: no remote copies, remote signals or barrier semaphores. Data moves between devices by JAX's collectives and lax.ppermute only.
A program may use at most 256 MiB of HBM per device.

```python
import jax
import jax.numpy as jnp
from jax import lax

D = 8192
H = 64
KVH = 8
HD = 128
R = 64
STEPS = 4
SEQS = 16
CACHE = 192
ADAPTER_SHARDS = 16


def draw_lengths(key, part):
    key = jax.random.fold_in(key, 11)
    values = jax.random.randint(key, (SEQS,), 1, CACHE + 1)
    where_full = jax.random.randint(jax.random.fold_in(key, 12), (), 0, SEQS)
    return values.at[where_full].set(CACHE).astype(jnp.int32)


def draw_cache_keys(key, part):
    key = jax.random.fold_in(key, 21)
    shape = (SEQS, CACHE, KVH * HD)
    base = jax.random.normal(key, shape, jnp.float32) * 1.5
    return jnp.clip(base, -64.0, 64.0).astype(jnp.bfloat16)


def steps_of(own_key, shape, split, least, high):
    loudness = 1.0
    for dim, blocks in split:
        draws = jax.random.uniform(jax.random.fold_in(jax.random.fold_in(own_key, 6), dim), (blocks,), jnp.float32, least / len(split), high / len(split))
        loudness = loudness * jnp.repeat(jnp.exp(draws), shape[dim] // blocks).reshape((-1,) + (1,) * (len(shape) - 1 - dim))
    return loudness


def gaussian(own_key, dims, scale, reach, split=(), held_as=jnp.bfloat16):
    result = scale * jax.random.normal(own_key, dims, jnp.float32)
    if split:
        result = result * steps_of(own_key, dims, split, -0.22, 0.18)
    return jnp.clip(result, -reach, reach).astype(held_as)


def setup_inputs(seed: int = 0, part: int = 0) -> dict:
    seeds = jax.random.split(jax.random.key(seed), 10)
    part_splits = jax.random.split(jax.random.fold_in(seeds[9], part), 10)
    tokens = gaussian(part_splits[0], (STEPS, SEQS, D), 1.0, 6.0, ((1, 4), (2, 4)))
    lengths = draw_lengths(jax.random.fold_in(jax.random.fold_in(seeds[9], part), 71), part)
    cache_keys = draw_cache_keys(jax.random.fold_in(jax.random.fold_in(seeds[9], part), 71), part)
    cache_values = gaussian(part_splits[3], (SEQS, CACHE, KVH * HD), 1.0, 6.0, ((0, 4), (1, 4)))
    q_weight = gaussian(seeds[4], (D, H * HD), D ** -0.5, 0.0625, ((0, 4), (1, 4)))
    kv_weight = gaussian(seeds[5], (D, 2 * KVH * HD), D ** -0.5, 0.0625, ((0, 4),))
    o_weight = gaussian(seeds[6], (H * HD, D), (H * HD) ** -0.5, 0.0625, ((0, 4), (1, 4)))
    adapters = gaussian(seeds[7], (4, R, D), (D // 8) ** -0.5, 0.1875, ((2, 16),))
    layout = jax.random.permutation(seeds[8], ADAPTER_SHARDS).astype(jnp.int32)
    return dict(tokens=tokens, lengths=lengths, cache_keys=cache_keys, cache_values=cache_values, q_weight=q_weight, kv_weight=kv_weight, o_weight=o_weight, adapters=adapters, layout=layout)


def reference(tokens, lengths, cache_keys, cache_values, q_weight, kv_weight, o_weight, adapters, layout):
    pieces = adapters.reshape(4, R, ADAPTER_SHARDS, D // ADAPTER_SHARDS)
    ordered = jnp.zeros_like(pieces).at[:, :, layout].set(pieces).reshape(4, R, D)
    q_merged = (q_weight.astype(jnp.float32) + jnp.dot(ordered[0].T, ordered[1], preferred_element_type=jnp.float32)).astype(jnp.bfloat16)
    o_merged = (o_weight.astype(jnp.float32) + jnp.dot(ordered[2].T, ordered[3], preferred_element_type=jnp.float32)).astype(jnp.bfloat16)
    flat = tokens.reshape(STEPS * SEQS, D)
    group = H // KVH
    queries = jnp.dot(flat, q_merged, preferred_element_type=jnp.float32).astype(jnp.bfloat16).reshape(STEPS, SEQS, KVH, group, HD)
    new_kv = jnp.dot(flat, kv_weight, preferred_element_type=jnp.float32).astype(jnp.bfloat16).reshape(STEPS, SEQS, 2, KVH, HD)
    scale = HD ** -0.5
    causal = jnp.arange(STEPS, dtype=jnp.int32)[:, None] >= jnp.arange(STEPS, dtype=jnp.int32)[None, :]

    def one_sequence(seq):
        query = queries[:, seq].astype(jnp.float32)
        keys = cache_keys[seq].reshape(CACHE, KVH, HD).astype(jnp.float32)
        values = cache_values[seq].reshape(CACHE, KVH, HD).astype(jnp.float32)
        new_keys = new_kv[:, seq, 0].astype(jnp.float32)
        new_values = new_kv[:, seq, 1].astype(jnp.float32)
        valid = jnp.arange(CACHE, dtype=jnp.int32) < lengths[seq]
        cache_scores = jnp.einsum("skgd,pkd->skgp", query, keys) * scale
        cache_scores = jnp.where(valid[None, None, None, :], cache_scores, -1e30)
        new_scores = jnp.einsum("skgd,tkd->skgt", query, new_keys) * scale
        new_scores = jnp.where(causal[:, None, None, :], new_scores, -1e30)
        scores = jnp.concatenate([cache_scores, new_scores], axis=-1)
        top = jnp.max(scores, axis=-1, keepdims=True)
        weights = jnp.exp(scores - top)
        total = jnp.sum(weights, axis=-1, keepdims=True)
        summed = jnp.einsum("skgp,pkd->skgd", weights[..., :CACHE], values) + jnp.einsum("skgt,tkd->skgd", weights[..., CACHE:], new_values)
        return (summed / total).reshape(STEPS, H * HD)

    attn = lax.map(one_sequence, jnp.arange(SEQS, dtype=jnp.int32))
    attn = jnp.transpose(attn, (1, 0, 2)).astype(jnp.bfloat16).reshape(STEPS * SEQS, H * HD)
    mixed = jnp.dot(attn, o_merged, preferred_element_type=jnp.float32).astype(jnp.bfloat16)
    return mixed.reshape(STEPS, SEQS, D)
```

```python
import functools

import jax
import jax.numpy as jnp
from jax import lax
from jax.experimental import pallas as pl
from jax.experimental.pallas import tpu as pltpu
from jax.sharding import PartitionSpec as P

HD = 128
F32 = jnp.float32
BF16 = jnp.bfloat16
SIDE = 4
MIB = 1 << 20


def along_tp(x, k):
    return lax.ppermute(x, "tp", [(i, (i + k) % SIDE) for i in range(SIDE)])


def across_dp(x, k):
    return lax.ppermute(x, "dp", [(i, i ^ k) for i in range(SIDE)])


def to_holder(x, m):
    pairs = [(t * SIDE + d, d * SIDE + (t ^ m)) for t in range(SIDE) for d in range(SIDE)]
    return lax.ppermute(x, ("tp", "dp"), pairs)


def all_blocks(x):
    rows = [x] + [along_tp(x, k) for k in range(1, SIDE)]
    blocks = []
    for row in rows:
        far = across_dp(row, 2)
        blocks += [row, across_dp(row, 1), far, across_dp(far, 1)]
    return rows, blocks


def block_slots(inverse, first, t, d):
    source = lax.dynamic_slice_in_dim(inverse, first, SIDE, 0)
    return ((t - source // SIDE) % SIDE) * SIDE + ((source % SIDE) ^ d)


def pick(slots_ref, blocks, down_ref, up_ref, sem, first_down, first_up):
    for n in range(2 * SIDE):
        factor, dst = (0, down_ref) if n < SIDE else (1, up_ref)
        for s, block in enumerate(blocks):

            @pl.when(slots_ref[n] == s)
            def _(block=block, factor=factor, dst=dst, n=n):
                pltpu.make_async_copy(block.at[factor], dst.at[n % SIDE], sem.at[n]).start()

    for n in range(2 * SIDE):
        factor, dst = (0, down_ref) if n < SIDE else (1, up_ref)
        pltpu.make_async_copy(blocks[0].at[factor], dst.at[n % SIDE], sem.at[n]).wait()


def merged_rows(w_ref, down_ref, up, i, width):
    delta = lax.dot_general(down_ref[i], up, (((0,), (0,)), ((), ())), preferred_element_type=F32)
    return (w_ref[i * width : (i + 1) * width, :].astype(F32) + delta).astype(BF16)


def merge_dot_kernel(slots_ref, *refs):
    blocks = refs[:16]
    w_ref, x0, x1, x2, x3, out_ref, down_ref, up_ref, x_ref, sem = refs[16:]
    step = pl.program_id(0)
    width = down_ref.shape[2]
    cols = w_ref.shape[1]
    rows = x0.shape[0]

    @pl.when(step == 0)
    def _():
        for k, piece in enumerate((x0, x1, x2, x3)):
            x_ref[k * rows : (k + 1) * rows, :] = piece[...]
        pick(slots_ref, blocks, down_ref, up_ref, sem, 0, 0)

    per = width // cols
    up = up_ref[step // per, :, pl.ds(pl.multiple_of((step % per) * cols, cols), cols)]
    total = jnp.zeros(out_ref.shape, F32)
    for i in range(SIDE):
        merged = merged_rows(w_ref, down_ref, up, i, width)
        total += jnp.dot(x_ref[:, i * width : (i + 1) * width], merged, preferred_element_type=F32)
    out_ref[...] = total


def merge_kernel(slots_ref, *refs):
    blocks = refs[:16]
    w_ref, out_ref, down_ref, up_ref, sem = refs[16:]
    step = pl.program_id(0)
    width = down_ref.shape[2]
    cols = w_ref.shape[1]

    @pl.when(step == 0)
    def _():
        pick(slots_ref, blocks, down_ref, up_ref, sem, 0, 0)

    per = width // cols
    up = up_ref[step // per, :, pl.ds(pl.multiple_of((step % per) * cols, cols), cols)]
    for i in range(SIDE):
        out_ref[i * width : (i + 1) * width, :] = merged_rows(w_ref, down_ref, up, i, width)


def merge_call(kernel, slots, blocks, weight, pieces, out_rows, out_dtype, cols):
    depth, width = weight.shape
    rank, piece_cols = blocks[0].shape[1:]
    any_spec = pl.BlockSpec(memory_space=pl.ANY)
    scratch = [
        pltpu.VMEM((SIDE, rank, piece_cols), BF16),
        pltpu.VMEM((SIDE, rank, piece_cols), BF16),
    ]
    if pieces:
        scratch.append(pltpu.VMEM((SIDE * pieces[0].shape[0], depth), BF16))
    scratch.append(pltpu.SemaphoreType.DMA((2 * SIDE,)))
    return pl.pallas_call(
        kernel,
        out_shape=jax.ShapeDtypeStruct((out_rows, width), out_dtype),
        grid_spec=pltpu.PrefetchScalarGridSpec(
            num_scalar_prefetch=1,
            grid=(width // cols,),
            in_specs=[any_spec] * 16
            + [pl.BlockSpec((depth, cols), lambda j, s: (0, j))]
            + [pl.BlockSpec(p.shape, lambda j, s: (0, 0)) for p in pieces],
            out_specs=pl.BlockSpec((out_rows, cols), lambda j, s: (0, j)),
            scratch_shapes=scratch,
        ),
        compiler_params=pltpu.CompilerParams(vmem_limit_bytes=24 * MIB),
        cost_estimate=pl.CostEstimate(
            flops=2 * depth * width * (rank + 64), bytes_accessed=2 * depth * width, transcendentals=0
        ),
    )(slots, *blocks, weight, *pieces)


def attention_kernel(qa_ref, qb_ref, n0, n1, n2, n3, c0, c1, c2, c3, bias_ref, fresh_bias_ref, out_ref):
    scale = HD ** (-0.5)
    rows = qa_ref.shape[0]
    kv_dev = c0.shape[2] // HD
    group = qa_ref.shape[1] // HD // kv_dev
    queries = (qa_ref[...] + qb_ref[...]).astype(BF16)
    fresh = (n0[...] + n1[...] + n2[...] + n3[...]).astype(BF16)
    contract_last = (((1,), (1,)), ((), ()))

    def scores_of(q, keys, bias):
        s = lax.dot_general(q, keys, contract_last, preferred_element_type=F32) * scale
        s = s.reshape(group, rows, s.shape[1]) + bias[None]
        return s.reshape(group * rows, s.shape[2])

    def weighted(weights, values):
        coarse = weights.astype(BF16)
        rest = (weights - coarse.astype(F32)).astype(BF16)
        return jnp.dot(coarse, values, preferred_element_type=F32) + jnp.dot(
            rest, values, preferred_element_type=F32
        )

    for h in range(kv_dev):
        lanes = slice(h * HD, (h + 1) * HD)
        q = jnp.concatenate(
            [queries[:, (h * group + g) * HD : (h * group + g + 1) * HD] for g in range(group)], axis=0
        )
        scores = [scores_of(q, c[0, :, lanes], bias_ref[k]) for k, c in enumerate((c0, c1, c2, c3))]
        scores.append(scores_of(q, fresh[:, lanes], fresh_bias_ref[...]))
        values = [c[1, :, lanes] for c in (c0, c1, c2, c3)]
        values.append(fresh[:, (kv_dev + h) * HD : (kv_dev + h + 1) * HD])
        top = functools.reduce(jnp.maximum, [jnp.max(s, axis=1, keepdims=True) for s in scores])
        weights = [jnp.exp(s - top) for s in scores]
        total = sum(jnp.sum(w, axis=1, keepdims=True) for w in weights)
        summed = sum(weighted(w, v) for w, v in zip(weights, values))
        attn = (summed / total).astype(BF16)
        for g in range(group):
            out_ref[:, (h * group + g) * HD : (h * group + g + 1) * HD] = attn[g * rows : (g + 1) * rows]


def out_kernel(turn_ref, a0, a1, a2, a3, w_ref, first_ref, rest_ref, x_ref):
    rows = a0.shape[0]

    @pl.when(pl.program_id(0) == 0)
    def _():
        for k, piece in enumerate((a0, a1, a2, a3)):
            at = pl.multiple_of((turn_ref[0] ^ k) * rows, rows)
            x_ref[pl.ds(at, rows), :] = piece[...]

    total = jnp.dot(x_ref[...], w_ref[...], preferred_element_type=F32)
    first_ref[...] = total[:rows]
    for m in range(1, SIDE):
        rest_ref[m - 1] = total[m * rows : (m + 1) * rows].astype(BF16)


def joined_2(array, axis, combine):
    everything = jax.tree.map(lambda part: lax.all_gather(part, axis), array)
    leading = jax.tree.map(lambda part: part[0], everything)

    def turn(k, so_far):
        return combine(so_far, jax.tree.map(lambda part: part[k], everything))

    return lax.fori_loop(1, lax.axis_size(axis), turn, leading)


def join_partials(first, second):
    top_a, total_a, summed_a = first
    top_b, total_b, summed_b = second
    top = jnp.maximum(top_a, top_b)
    factor_a = jnp.exp(top_a - top)
    factor_b = jnp.exp(top_b - top)
    return (
        top,
        total_a * factor_a + total_b * factor_b,
        summed_a * factor_a[..., None] + summed_b * factor_b[..., None],
    )


def pick_columns(stacked, inverse, factor, start, count):
    piece_cols = stacked.shape[3]
    block_ids = lax.dynamic_slice_in_dim(inverse, start // piece_cols, count // piece_cols, 0)
    chosen = jnp.take(stacked[factor], block_ids, axis=1)
    return chosen.reshape(stacked.shape[1], count)


def general(
    tokens, lengths, cache_keys, cache_values, q_weight, kv_weight, o_weight, adapters, layout
):
    tp_index = lax.axis_index("tp")
    dp_index = lax.axis_index("dp")
    steps, seq_dev, feat_dev = tokens.shape
    rank = adapters.shape[1]
    shards = layout.shape[0]
    rows = steps * seq_dev
    scale = HD ** (-0.5)
    gathered = lax.all_gather(adapters, ("tp", "dp"), axis=2, tiled=True)
    width = gathered.shape[2]
    piece_cols = width // shards
    stacked = gathered.reshape(4, rank, shards, piece_cols)
    block_numbers = jnp.arange(shards, dtype=jnp.int32)
    inverse = jnp.sum(
        jnp.where(layout[None, :] == block_numbers[:, None], block_numbers[None, :], 0), axis=1
    )
    kv_part = jnp.dot(tokens.reshape(rows, feat_dev), kv_weight, preferred_element_type=jnp.float32)
    new_kv = lax.psum(kv_part, "tp").astype(jnp.bfloat16)
    full_tokens = lax.all_gather(tokens, "tp", axis=2, tiled=True)
    q_rows = q_weight.shape[0]
    q_cols = q_weight.shape[1]
    o_cols = o_weight.shape[1]
    col_start = tp_index * q_cols
    q_down_part = pick_columns(stacked, inverse, 0, dp_index * q_rows, q_rows)
    q_up_part = pick_columns(stacked, inverse, 1, col_start, q_cols)
    o_down_part = pick_columns(stacked, inverse, 2, col_start, q_cols)
    o_up_part = pick_columns(stacked, inverse, 3, dp_index * o_cols, o_cols)
    q_merged = (
        q_weight.astype(jnp.float32)
        + jnp.einsum("rf,rc->fc", q_down_part, q_up_part, preferred_element_type=jnp.float32)
    ).astype(jnp.bfloat16)
    o_merged = (
        o_weight.astype(jnp.float32)
        + jnp.einsum("rf,rc->fc", o_down_part, o_up_part, preferred_element_type=jnp.float32)
    ).astype(jnp.bfloat16)
    flat_tokens = full_tokens.reshape(rows, width)
    q_total = jnp.dot(
        flat_tokens,
        lax.all_gather(q_merged, "dp", axis=0, tiled=True),
        preferred_element_type=jnp.float32,
    )
    queries = q_total.astype(jnp.bfloat16).reshape(steps, seq_dev, q_cols)
    all_queries = lax.all_gather(queries, "tp", axis=2, tiled=True)
    heads = all_queries.shape[2] // HD
    kv_heads = cache_keys.shape[2] // HD
    group = heads // kv_heads
    head_dev = q_cols // HD
    span = cache_keys.shape[1]
    grouped = all_queries.reshape(steps, seq_dev, kv_heads, group, HD)
    keys_local = cache_keys.reshape(seq_dev, span, kv_heads, HD)
    values_local = cache_values.reshape(seq_dev, span, kv_heads, HD)
    positions = tp_index * span + jnp.arange(span, dtype=jnp.int32)
    valid = (positions[None, :] < lengths[:, None])[None, :, None, None, :]
    scores = (
        jnp.einsum("sbkgd,bpkd->sbkgp", grouped, keys_local, preferred_element_type=jnp.float32)
        * scale
    )
    scores = jnp.where(valid, scores, -1e30)
    local_top = jnp.max(scores, axis=-1)
    weights = jnp.where(valid, jnp.exp(scores - local_top[..., None]), 0.0)
    local_total = jnp.sum(weights, axis=-1).reshape(steps, seq_dev, heads)
    local_sum = jnp.einsum("sbkgp,bpkd->sbkgd", weights, values_local.astype(jnp.float32)).reshape(
        steps, seq_dev, heads, HD
    )
    local_top = local_top.reshape(steps, seq_dev, heads)
    joined = joined_2((local_top, local_total, local_sum), "tp", join_partials)
    own_top = lax.dynamic_slice_in_dim(joined[0], tp_index * head_dev, head_dev, 2)
    own_total = lax.dynamic_slice_in_dim(joined[1], tp_index * head_dev, head_dev, 2)
    own_sum = lax.dynamic_slice_in_dim(joined[2], tp_index * head_dev, head_dev, 2)
    fresh = new_kv.reshape(steps, seq_dev, 2, kv_heads, HD)
    fresh_keys = lax.dynamic_slice_in_dim(
        jnp.repeat(fresh[:, :, 0], group, axis=2), tp_index * head_dev, head_dev, 2
    )
    fresh_values = lax.dynamic_slice_in_dim(
        jnp.repeat(fresh[:, :, 1], group, axis=2), tp_index * head_dev, head_dev, 2
    )
    own_queries = queries.reshape(steps, seq_dev, head_dev, HD)
    fresh_scores = (
        jnp.einsum("sbhd,tbhd->sbht", own_queries, fresh_keys, preferred_element_type=jnp.float32)
        * scale
    )
    causal = (
        jnp.arange(steps, dtype=jnp.int32)[:, None] >= jnp.arange(steps, dtype=jnp.int32)[None, :]
    )[:, None, None, :]
    fresh_scores = jnp.where(causal, fresh_scores, -1e30)
    top = jnp.maximum(own_top, jnp.max(fresh_scores, axis=-1))
    cache_factor = jnp.exp(own_top - top)
    fresh_weights = jnp.exp(fresh_scores - top[..., None])
    total = own_total * cache_factor + jnp.sum(fresh_weights, axis=-1)
    summed = own_sum * cache_factor[..., None] + jnp.einsum(
        "sbht,tbhd->sbhd", fresh_weights, fresh_values.astype(jnp.float32)
    )
    attn = (summed / total[..., None]).astype(jnp.bfloat16).reshape(rows, q_cols)
    blocks_in = o_cols // q_cols
    out_blocks = o_merged.reshape(q_cols, blocks_in, q_cols)
    partial_out = jnp.einsum(
        "snc,cjf->jnsf",
        lax.all_gather(attn.reshape(steps, seq_dev, q_cols), "dp", axis=1, tiled=True),
        out_blocks,
        preferred_element_type=jnp.float32,
    )
    dp_size = lax.axis_size("dp")
    tp_size = lax.axis_size("tp")
    arranged = partial_out.reshape(blocks_in * dp_size, seq_dev, steps, q_cols)
    spread_terms = jnp.zeros((tp_size * dp_size, seq_dev, steps, q_cols), jnp.float32)
    spread_terms = lax.dynamic_update_slice_in_dim(
        spread_terms, arranged, dp_index * blocks_in * dp_size, 0
    )
    own_rows = lax.psum_scatter(spread_terms, ("tp", "dp"), scatter_dimension=0, tiled=True)
    mixed = jnp.transpose(own_rows.reshape(seq_dev, steps, q_cols), (1, 0, 2)).astype(jnp.bfloat16)
    return mixed


def on_device(
    tokens, lengths, cache_keys, cache_values, q_weight, kv_weight, o_weight, adapters, layout
):
    t = lax.axis_index("tp")
    d = lax.axis_index("dp")
    steps, seq_dev, feat_dev = tokens.shape
    rows = steps * seq_dev
    span = cache_keys.shape[1]
    kv_cols = cache_keys.shape[2] // SIDE
    shards = layout.shape[0]
    numbers = jnp.arange(shards, dtype=jnp.int32)
    inverse = jnp.sum(jnp.where(layout[None, :] == numbers[:, None], numbers[None, :], 0), axis=1)
    of_d = block_slots(inverse, d * SIDE, t, d)
    of_t = block_slots(inverse, t * SIDE, t, d)
    q_slots = jnp.concatenate([of_d, of_t])
    o_slots = jnp.concatenate([of_t, of_d])
    own = tokens.reshape(rows, feat_dev)

    q_rows, q_blocks = all_blocks(adapters[:2])

    by_feature = jnp.stack([own] + [along_tp(own, k) for k in range(1, SIDE)])

    def features(block):
        return lax.dynamic_index_in_dim(by_feature, (t - block) % SIDE, 0, keepdims=False)

    pieces = [features(d)] + [across_dp(features(d ^ k), k) for k in range(1, SIDE)]

    kv_part = jnp.dot(own, kv_weight, preferred_element_type=F32)

    def kv_of(head):
        halves = [
            lax.dynamic_slice_in_dim(kv_part, base + head * kv_cols, kv_cols, 1)
            for base in (0, kv_cols * SIDE)
        ]
        return jnp.concatenate(halves, axis=1)

    kv_terms = [kv_of(t)] + [along_tp(kv_of((t + k) % SIDE), k) for k in range(1, SIDE)]

    cache = jnp.stack([cache_keys, cache_values]).reshape(2, seq_dev * span, SIDE * kv_cols)

    def cache_of(head):
        return lax.dynamic_slice_in_dim(cache, head * kv_cols, kv_cols, 2)

    caches = [cache_of(t)] + [along_tp(cache_of((t + k) % SIDE), k) for k in range(1, SIDE)]
    o_rows, o_blocks = all_blocks(adapters[2:])

    q_part = merge_call(merge_dot_kernel, q_slots, q_blocks, q_weight, pieces, SIDE * rows, F32, 256)
    near = across_dp(jnp.concatenate([q_part[rows : 2 * rows], q_part[3 * rows :]]), 1)
    q_near = q_part[:rows] + near[:rows]
    q_far = across_dp(q_part[2 * rows : 3 * rows] + near[rows:], 2)

    seq_of_row = jnp.arange(rows, dtype=jnp.int32) % seq_dev
    step_of_row = jnp.arange(rows, dtype=jnp.int32) // seq_dev
    column = jnp.arange(seq_dev * span, dtype=jnp.int32)
    came_from = (t - jnp.arange(SIDE, dtype=jnp.int32)) % SIDE
    position = came_from[:, None] * span + (column % span)[None, :]
    inside = position < jnp.repeat(lengths, span)[None, :]
    same = (column // span)[None, :] == seq_of_row[:, None]
    bias = jnp.where(inside[:, None, :] & same[None], 0.0, -1e30).astype(F32)
    causal = (step_of_row[None, :] <= step_of_row[:, None]) & (seq_of_row[None, :] == seq_of_row[:, None])
    fresh_bias = jnp.where(causal, 0.0, -1e30).astype(F32)

    attn = pl.pallas_call(
        attention_kernel,
        out_shape=jax.ShapeDtypeStruct((rows, q_weight.shape[1]), BF16),
        compiler_params=pltpu.CompilerParams(vmem_limit_bytes=16 * MIB),
    )(q_near, q_far, *kv_terms, *caches, bias, fresh_bias)

    o_merged = merge_call(merge_kernel, o_slots, o_blocks, o_weight, [], o_weight.shape[0], BF16, 256)
    attn_rows = [attn] + [across_dp(attn, k) for k in range(1, SIDE)]
    depth, width = o_weight.shape
    cols = 512
    first, rest = pl.pallas_call(
        out_kernel,
        out_shape=(
            jax.ShapeDtypeStruct((rows, width), F32),
            jax.ShapeDtypeStruct((SIDE - 1, rows, width), BF16),
        ),
        grid_spec=pltpu.PrefetchScalarGridSpec(
            num_scalar_prefetch=1,
            grid=(width // cols,),
            in_specs=[pl.BlockSpec((rows, depth), lambda j, s: (0, 0))] * SIDE
            + [pl.BlockSpec((depth, cols), lambda j, s: (0, j))],
            out_specs=(
                pl.BlockSpec((rows, cols), lambda j, s: (0, j)),
                pl.BlockSpec((SIDE - 1, rows, cols), lambda j, s: (0, 0, j)),
            ),
            scratch_shapes=[pltpu.VMEM((SIDE * rows, depth), BF16)],
        ),
        compiler_params=pltpu.CompilerParams(vmem_limit_bytes=16 * MIB),
    )((t ^ d).reshape(1), *attn_rows, o_merged)
    mixed = to_holder(first, 0)
    for m in range(1, SIDE):
        mixed = mixed + to_holder(rest[m - 1], m).astype(F32)
    return mixed.astype(BF16).reshape(steps, seq_dev, width)


def solution(mesh):
    def fits(layout, cache_keys):
        sides = mesh.shape["tp"] == SIDE and mesh.shape["dp"] == SIDE
        return sides and layout.shape[0] == SIDE * SIDE

    def run(tokens, lengths, cache_keys, cache_values, q_weight, kv_weight, o_weight, adapters, layout):
        body = on_device if fits(layout, cache_keys) else general
        return body(
            tokens, lengths, cache_keys, cache_values, q_weight, kv_weight, o_weight, adapters, layout
        )

    return jax.shard_map(
        run,
        mesh=mesh,
        in_specs=(
            P(None, ("groups", "dp"), "tp"),
            P(("groups", "dp")),
            P(("groups", "dp"), "tp", None),
            P(("groups", "dp"), "tp", None),
            P("dp", "tp"),
            P("tp", None),
            P("tp", "dp"),
            P(None, None, ("tp", "dp")),
            P(),
        ),
        out_specs=P(None, ("groups", "dp"), "tp"),
        check_vma=False,
    )
```

```python
import functools

import jax
import jax.numpy as jnp
from jax import lax
from jax.experimental import pallas as pl
from jax.experimental.pallas import tpu as pltpu
from jax.sharding import PartitionSpec as P

HD = 128
F32 = jnp.float32
BF16 = jnp.bfloat16
SIDE = 4
BLOCK = 256
PACK_COST = 64
MIB = 1 << 20


def after(x, *earlier):
    return lax.optimization_barrier((x, *earlier))[0]


def along_tp(x, k):
    return lax.ppermute(x, "tp", [(i, (i + k) % SIDE) for i in range(SIDE)])


def across_dp(x, k):
    return lax.ppermute(x, "dp", [(i, i ^ k) for i in range(SIDE)])


def across_groups(x):
    return lax.ppermute(x, "groups", [(0, 1), (1, 0)])


def to_holder(x, m):
    pairs = [(t * SIDE + d, d * SIDE + (t ^ m)) for t in range(SIDE) for d in range(SIDE)]
    return lax.ppermute(x, ("tp", "dp"), pairs)


def pack_kernel(*refs):
    out_ref, at = refs[-1], 0
    for ref in refs[:-1]:
        out_ref[at : at + ref.shape[0]] = ref[...]
        at += ref.shape[0]


def pack(parts, cost=1):
    spec = pl.BlockSpec(memory_space=pltpu.VMEM)
    shape = (sum(part.shape[0] for part in parts), *parts[0].shape[1:])
    return pl.pallas_call(
        pack_kernel,
        out_shape=jax.ShapeDtypeStruct(shape, parts[0].dtype),
        in_specs=[spec] * len(parts),
        out_specs=spec,
        compiler_params=pltpu.CompilerParams(vmem_limit_bytes=4 * MIB),
        cost_estimate=pl.CostEstimate(flops=0, bytes_accessed=cost * MIB, transcendentals=0),
    )(*parts)


def small_call(kernel, scalars, arrays, out_shape, vmem=8 * MIB):
    spec = pl.BlockSpec(memory_space=pltpu.VMEM)
    return pl.pallas_call(
        kernel,
        out_shape=out_shape,
        in_specs=[pl.BlockSpec(memory_space=pltpu.SMEM)] + [spec] * len(arrays),
        out_specs=jax.tree.map(lambda _: spec, out_shape),
        compiler_params=pltpu.CompilerParams(vmem_limit_bytes=vmem),
    )(scalars, *arrays)


def first_kernel(y_ref, adapters_ref, tokens_ref, out_ref):
    half = adapters_ref.shape[2]
    width = out_ref.shape[1]
    rows = tokens_ref.shape[0]
    for f in range(4):
        out_ref[f * half : (f + 1) * half] = adapters_ref[f, y_ref[0]]
    for j in range(tokens_ref.shape[1] // width):
        at = 4 * half + j * rows
        out_ref[at : at + rows] = tokens_ref[:, j * width : (j + 1) * width]


def sort_kernel(from_ref, *refs):
    held, (q_ref, o_ref, across_ref, *sends) = refs[:SIDE], refs[SIDE:]
    half = q_ref.shape[1]
    others = SIDE - 1
    for k in range(1, SIDE):
        for f in range(2):
            unit = held[k][f * half : (f + 1) * half]
            q_ref[f * others + k - 1] = unit
            across_ref[f * others + k - 1] = unit
            o_ref[f * others + k - 1] = held[k][(2 + f) * half : (3 + f) * half]
    slab = sends[0].shape[0]
    for k in range(SIDE):
        for j, ref in enumerate(held):

            @pl.when(from_ref[k] == j)
            def _(ref=ref, k=k):
                for u in range(slab):
                    unit = ref[(4 + u) * half : (5 + u) * half]
                    if k < 2:
                        sends[k][u] = unit
                    else:
                        across_ref[2 * others + (k - 2) * slab + u] = unit


def split_kernel(heads_ref, tokens_ref, keys_ref, values_ref, w_hbm, *refs):
    outs, (w_ref, kv_ref, sem) = refs[:SIDE], refs[SIDE:]
    row_parts = row_copies(w_hbm, w_ref, sem)
    for copy in row_parts:
        copy.start()
    cached = keys_ref.shape[0]
    rows, width = kv_ref.shape
    cols = outs[0].shape[1]
    places = [pl.multiple_of(heads_ref[k] * cols, cols) for k in range(SIDE)]
    for at, out in zip(places, outs):
        out[:cached] = keys_ref[:, pl.ds(at, cols)]
        out[cached : 2 * cached] = values_ref[:, pl.ds(at, cols)]
    for i in range(0, w_ref.shape[0], BLOCK):
        row_parts[i // BLOCK].wait()
        lanes = slice(i, i + BLOCK)
        term = jnp.dot(tokens_ref[:, lanes], w_ref[lanes, :], preferred_element_type=F32)
        if i == 0:
            kv_ref[...] = term
        else:
            kv_ref[...] += term
    for at, out in zip(places, outs):
        for part in range(2):
            term = kv_ref[:, pl.ds(pl.multiple_of(part * (width // 2) + at, cols), cols)]
            coarse = term.astype(BF16)
            row = 2 * cached + part * rows
            out[row : row + rows] = coarse
            out[row + 2 * rows : row + 3 * rows] = (term - coarse.astype(F32)).astype(BF16)


def split_call(heads, own, keys, values, weight, out_shape):
    spec = pl.BlockSpec(memory_space=pltpu.VMEM)
    return pl.pallas_call(
        split_kernel,
        out_shape=[out_shape] * SIDE,
        in_specs=[pl.BlockSpec(memory_space=pltpu.SMEM)]
        + [spec] * 3
        + [pl.BlockSpec(memory_space=pl.ANY)],
        out_specs=[spec] * SIDE,
        scratch_shapes=[
            pltpu.VMEM(weight.shape, BF16),
            pltpu.VMEM((own.shape[0], weight.shape[1]), F32),
            pltpu.SemaphoreType.DMA((weight.shape[0] // BLOCK,)),
        ],
        compiler_params=pltpu.CompilerParams(vmem_limit_bytes=16 * MIB),
        cost_estimate=pl.CostEstimate(
            flops=2 * own.size * weight.shape[1], bytes_accessed=4 * weight.size, transcendentals=0
        ),
    )(heads, own, keys, values, pltpu.with_memory_space_constraint(weight, pltpu.HBM))


def corners_of(mine_far, other):
    half = other.shape[0] // 2
    return [across_dp(other[:half], 2), across_groups(mine_far[half : 2 * half])]


def with_sibling(packed, corners):
    near = [packed, *corners]
    return near + [across_dp(x, 1) for x in near]


def block_places(inverse, first, t, d):
    source = lax.dynamic_slice_in_dim(inverse, first, SIDE, 0)
    return (t - source // SIDE) % SIDE, (source % SIDE) ^ d


def pick(slots_ref, parts, other_at, down_ref, up_ref, sem):
    y = slots_ref[4 * SIDE]
    half = down_ref.shape[0] // 2
    cols = down_ref.shape[1] // SIDE
    others = SIDE - 1

    def copy(n, source, h):
        dst = down_ref if n < SIDE else up_ref
        at = pl.multiple_of(h * half, half)
        lanes = pl.ds((n % SIDE) * cols, cols)
        return pltpu.make_async_copy(source, dst.at[pl.ds(at, half), lanes], sem.at[2 * n + h])

    for n in range(2 * SIDE):
        factor = n // SIDE
        row, across = slots_ref[n], slots_ref[2 * SIDE + n]
        far = across >> 1
        in_row = factor * others + row - 1
        at_mine = jnp.where(row == 0, far * 4 + factor * 2 + y, 8 + far * 2 * others + in_row)
        at_other = jnp.where(row == 0, far * 4 + factor * 2 + 1 - y, other_at + in_row)
        corner = (far == 1) & (row > 0)
        for side in range(2):
            packed, *corners = parts[side * 3 : side * 3 + 3]
            here = (across & 1) == side

            @pl.when(here)
            def _(packed=packed, at_mine=at_mine, n=n):
                copy(n, packed.at[at_mine], y).start()

            @pl.when(here & jnp.logical_not(corner))
            def _(packed=packed, at_other=at_other, n=n):
                copy(n, packed.at[at_other], 1 - y).start()

            @pl.when(here & corner)
            def _(source=corners[factor], row=row, n=n):
                copy(n, source.at[row - 1], 1 - y).start()

    for n in range(2 * SIDE):
        for h in range(2):
            copy(n, parts[0].at[0], h).wait()


def merged_rows(w, down_ref, up_ref, lanes):
    delta = lax.dot_general(
        down_ref[:, lanes], up_ref[...], (((0,), (0,)), ((), ())), preferred_element_type=F32
    )
    return (w.astype(F32) + delta).astype(BF16)


def row_copies(src, dst, sem):
    return [
        pltpu.make_async_copy(src.at[pl.ds(i, BLOCK)], dst.at[pl.ds(i, BLOCK)], sem.at[i // BLOCK])
        for i in range(0, src.shape[0], BLOCK)
    ]


def place_rows(turn, pieces, x_ref):
    rows = pieces[0].shape[0]
    for m, piece in enumerate(pieces):
        x_ref[pl.ds(pl.multiple_of((turn ^ m) * rows, rows), rows), :] = piece[...]


def merge_dot_kernel(slots_ref, *refs):
    parts = refs[:6]
    w_hbm, own_ref, across_ref, out_ref, down_ref, up_ref, w_ref, x_ref, tokens_ref = refs[6:15]
    sem, token_sem, row_sem = refs[15:]
    slab, half, width = own_ref.shape
    total = parts[3].shape[0]
    at = 2 * (SIDE - 1)
    sources = [
        own_ref,
        parts[3].at[pl.ds(total - slab, slab)],
        across_ref.at[pl.ds(at, slab)],
        parts[3].at[pl.ds(total - 2 * slab - at, slab)],
    ]
    copies = [
        pltpu.make_async_copy(source, tokens_ref.at[pl.ds(k * slab, slab)], token_sem.at[k])
        for k, source in enumerate(sources)
    ]
    row_parts = row_copies(w_hbm, w_ref, row_sem)
    for copy in copies + row_parts:
        copy.start()
    pick(slots_ref, parts, total - slab - at, down_ref, up_ref, sem)
    for copy in copies:
        copy.wait()
    rows = slab * half * width // x_ref.shape[1]
    for k in range(SIDE):
        for j in range(x_ref.shape[1] // width):
            u, row = divmod(j * rows, half)
            term = tokens_ref[k * slab + u, row : row + rows, :]
            x_ref[k * rows : (k + 1) * rows, j * width : (j + 1) * width] = term
    for i in range(0, w_ref.shape[0], BLOCK):
        row_parts[i // BLOCK].wait()
        lanes = slice(i, i + BLOCK)
        merged = merged_rows(w_ref[lanes, :], down_ref, up_ref, lanes)
        term = jnp.dot(x_ref[:, lanes], merged, preferred_element_type=F32)
        if i == 0:
            out_ref[...] = term
        else:
            out_ref[...] += term


def merge_kernel(slots_ref, *refs):
    w_ref, out_ref, down_ref, up_ref, sem, row_sem = refs[6:]
    copies = row_copies(w_ref, out_ref, row_sem)
    for copy in copies:
        copy.start()
    pick(slots_ref, refs[:6], refs[0].shape[0] - 2 * (SIDE - 1), down_ref, up_ref, sem)
    for i in range(0, w_ref.shape[0], BLOCK):
        copies[i // BLOCK].wait()
        lanes = slice(i, i + BLOCK)
        out_ref[lanes, :] = merged_rows(out_ref[lanes, :], down_ref, up_ref, lanes)


def merge_call(kernel, slots, parts, weight, pieces, out_shape, sems, rank, cost):
    depth, width = weight.shape
    piece_cols = parts[0].shape[-1]
    vmem_spec = pl.BlockSpec(memory_space=pltpu.VMEM)
    scratch = [pltpu.VMEM((rank, SIDE * piece_cols), BF16)] * 2
    if pieces:
        scratch.append(pltpu.VMEM(weight.shape, BF16))
        scratch.append(pltpu.VMEM((out_shape.shape[0], depth), BF16))
        slab, *unit = pieces[0].shape
        scratch.append(pltpu.VMEM((SIDE * slab, *unit), BF16))
    scratch += [pltpu.SemaphoreType.DMA((count,)) for count in sems]
    return pl.pallas_call(
        kernel,
        out_shape=out_shape,
        in_specs=[pl.BlockSpec(memory_space=pltpu.SMEM)]
        + [pl.BlockSpec(memory_space=pl.ANY)] * len(parts)
        + [pl.BlockSpec(memory_space=pl.ANY)]
        + [vmem_spec] * len(pieces),
        out_specs=vmem_spec,
        scratch_shapes=scratch,
        compiler_params=pltpu.CompilerParams(vmem_limit_bytes=16 * MIB),
        cost_estimate=pl.CostEstimate(flops=0, bytes_accessed=cost * MIB, transcendentals=0),
    )(slots, *parts, weight, *pieces)


def attention_kernel(seqs, spots_ref, qa_ref, qb_ref, c0, c1, c3, keys_ref, rest_ref, out_ref):
    scale = HD ** (-0.5)
    rows = qa_ref.shape[0]
    kv_dev = c0.shape[1] // HD
    group = qa_ref.shape[1] // HD // kv_dev
    span = (c0.shape[0] - 4 * rows) // (2 * seqs)
    cached = seqs * span
    queries = (qa_ref[...] + qb_ref[...]).astype(BF16)

    row_seq = lax.broadcasted_iota(jnp.int32, (rows, cached), 0) % seqs
    column = lax.broadcasted_iota(jnp.int32, (rows, cached), 1)
    biases = []
    for k in range(SIDE):
        valid = column < 0
        for b in range(seqs):
            left = jnp.clip(spots_ref[SIDE + b] - spots_ref[k] * span, 0, span)
            inside = (column >= b * span) & (column < b * span + left)
            valid |= inside & (row_seq == b)
        biases.append(jnp.where(valid, 0.0, -1e30))
    row = lax.broadcasted_iota(jnp.int32, (rows, rows), 0)
    earlier = lax.broadcasted_iota(jnp.int32, (rows, rows), 1)
    causal = (earlier // seqs <= row // seqs) & (earlier % seqs == row % seqs)
    fresh_bias = jnp.where(causal, 0.0, -1e30)

    def fresh_part(part):
        terms = []
        for c in (c0, c1, rest_ref, c3):
            at = c.shape[0] - 4 * rows + part * rows
            terms.append(c[at : at + rows].astype(F32))
            terms.append(c[at + 2 * rows : at + 3 * rows].astype(F32))
        return sum(terms).astype(BF16)

    fresh_keys, fresh_values = fresh_part(0), fresh_part(1)
    contract_last = (((1,), (1,)), ((), ()))

    def scores_of(q, keys, bias):
        s = lax.dot_general(q, keys, contract_last, preferred_element_type=F32) * scale
        s = s.reshape(group, rows, s.shape[1]) + bias[None]
        return s.reshape(group * rows, s.shape[2])

    def weighted(weights, values):
        coarse = weights.astype(BF16)
        rest = (weights - coarse.astype(F32)).astype(BF16)
        return jnp.dot(coarse, values, preferred_element_type=F32) + jnp.dot(
            rest, values, preferred_element_type=F32
        )

    for h in range(kv_dev):
        lanes = slice(h * HD, (h + 1) * HD)
        q = jnp.concatenate(
            [queries[:, (h * group + g) * HD : (h * group + g + 1) * HD] for g in range(group)], axis=0
        )
        scores = [scores_of(q, c[:cached, lanes], biases[k]) for k, c in enumerate((c0, c1, keys_ref, c3))]
        scores.append(scores_of(q, fresh_keys[:, lanes], fresh_bias))
        values = [c[cached : 2 * cached, lanes] for c in (c0, c1)]
        values += [rest_ref[:cached, lanes], c3[cached : 2 * cached, lanes]]
        values.append(fresh_values[:, lanes])
        top = functools.reduce(jnp.maximum, [jnp.max(s, axis=1, keepdims=True) for s in scores])
        weights = [jnp.exp(s - top) for s in scores]
        total = sum(jnp.sum(w, axis=1, keepdims=True) for w in weights)
        summed = sum(weighted(w, v) for w, v in zip(weights, values))
        attn = (summed / total).astype(BF16)
        for g in range(group):
            out_ref[:, (h * group + g) * HD : (h * group + g + 1) * HD] = attn[g * rows : (g + 1) * rows]


def out_kernel(turn_ref, a0, a1, a2, a3, w_ref, first_ref, rest_ref, x_ref):
    rows = a0.shape[0]
    place_rows(turn_ref[0], (a0, a1, a2, a3), x_ref)
    for j in range(0, w_ref.shape[1], 2 * BLOCK):
        lanes = slice(j, j + 2 * BLOCK)
        total = jnp.dot(x_ref[...], w_ref[:, lanes], preferred_element_type=F32)
        first_ref[:, lanes] = total[:rows]
        for m in range(1, SIDE):
            rest_ref[m - 1, :, lanes] = total[m * rows : (m + 1) * rows].astype(BF16)


def joined_2(array, axis, combine):
    everything = jax.tree.map(lambda part: lax.all_gather(part, axis), array)
    leading = jax.tree.map(lambda part: part[0], everything)

    def turn(k, so_far):
        return combine(so_far, jax.tree.map(lambda part: part[k], everything))

    return lax.fori_loop(1, lax.axis_size(axis), turn, leading)


def join_partials(first, second):
    top_a, total_a, summed_a = first
    top_b, total_b, summed_b = second
    top = jnp.maximum(top_a, top_b)
    factor_a = jnp.exp(top_a - top)
    factor_b = jnp.exp(top_b - top)
    return (
        top,
        total_a * factor_a + total_b * factor_b,
        summed_a * factor_a[..., None] + summed_b * factor_b[..., None],
    )


def pick_columns(stacked, inverse, factor, start, count):
    piece_cols = stacked.shape[3]
    block_ids = lax.dynamic_slice_in_dim(inverse, start // piece_cols, count // piece_cols, 0)
    chosen = jnp.take(stacked[factor], block_ids, axis=1)
    return chosen.reshape(stacked.shape[1], count)


def general(
    tokens, lengths, cache_keys, cache_values, q_weight, kv_weight, o_weight, adapters, layout
):
    tp_index = lax.axis_index("tp")
    dp_index = lax.axis_index("dp")
    steps, seq_dev, feat_dev = tokens.shape
    rank = adapters.shape[1]
    shards = layout.shape[0]
    rows = steps * seq_dev
    scale = HD ** (-0.5)
    gathered = lax.all_gather(adapters, ("tp", "dp"), axis=2, tiled=True)
    width = gathered.shape[2]
    piece_cols = width // shards
    stacked = gathered.reshape(4, rank, shards, piece_cols)
    block_numbers = jnp.arange(shards, dtype=jnp.int32)
    inverse = jnp.sum(
        jnp.where(layout[None, :] == block_numbers[:, None], block_numbers[None, :], 0), axis=1
    )
    kv_part = jnp.dot(tokens.reshape(rows, feat_dev), kv_weight, preferred_element_type=jnp.float32)
    new_kv = lax.psum(kv_part, "tp").astype(jnp.bfloat16)
    full_tokens = lax.all_gather(tokens, "tp", axis=2, tiled=True)
    q_rows = q_weight.shape[0]
    q_cols = q_weight.shape[1]
    o_cols = o_weight.shape[1]
    col_start = tp_index * q_cols
    q_down_part = pick_columns(stacked, inverse, 0, dp_index * q_rows, q_rows)
    q_up_part = pick_columns(stacked, inverse, 1, col_start, q_cols)
    o_down_part = pick_columns(stacked, inverse, 2, col_start, q_cols)
    o_up_part = pick_columns(stacked, inverse, 3, dp_index * o_cols, o_cols)
    q_merged = (
        q_weight.astype(jnp.float32)
        + jnp.einsum("rf,rc->fc", q_down_part, q_up_part, preferred_element_type=jnp.float32)
    ).astype(jnp.bfloat16)
    o_merged = (
        o_weight.astype(jnp.float32)
        + jnp.einsum("rf,rc->fc", o_down_part, o_up_part, preferred_element_type=jnp.float32)
    ).astype(jnp.bfloat16)
    flat_tokens = full_tokens.reshape(rows, width)
    q_total = jnp.dot(
        flat_tokens,
        lax.all_gather(q_merged, "dp", axis=0, tiled=True),
        preferred_element_type=jnp.float32,
    )
    queries = q_total.astype(jnp.bfloat16).reshape(steps, seq_dev, q_cols)
    all_queries = lax.all_gather(queries, "tp", axis=2, tiled=True)
    heads = all_queries.shape[2] // HD
    kv_heads = cache_keys.shape[2] // HD
    group = heads // kv_heads
    head_dev = q_cols // HD
    span = cache_keys.shape[1]
    grouped = all_queries.reshape(steps, seq_dev, kv_heads, group, HD)
    keys_local = cache_keys.reshape(seq_dev, span, kv_heads, HD)
    values_local = cache_values.reshape(seq_dev, span, kv_heads, HD)
    positions = tp_index * span + jnp.arange(span, dtype=jnp.int32)
    valid = (positions[None, :] < lengths[:, None])[None, :, None, None, :]
    scores = (
        jnp.einsum("sbkgd,bpkd->sbkgp", grouped, keys_local, preferred_element_type=jnp.float32)
        * scale
    )
    scores = jnp.where(valid, scores, -1e30)
    local_top = jnp.max(scores, axis=-1)
    weights = jnp.where(valid, jnp.exp(scores - local_top[..., None]), 0.0)
    local_total = jnp.sum(weights, axis=-1).reshape(steps, seq_dev, heads)
    local_sum = jnp.einsum("sbkgp,bpkd->sbkgd", weights, values_local.astype(jnp.float32)).reshape(
        steps, seq_dev, heads, HD
    )
    local_top = local_top.reshape(steps, seq_dev, heads)
    joined = joined_2((local_top, local_total, local_sum), "tp", join_partials)
    own_top = lax.dynamic_slice_in_dim(joined[0], tp_index * head_dev, head_dev, 2)
    own_total = lax.dynamic_slice_in_dim(joined[1], tp_index * head_dev, head_dev, 2)
    own_sum = lax.dynamic_slice_in_dim(joined[2], tp_index * head_dev, head_dev, 2)
    fresh = new_kv.reshape(steps, seq_dev, 2, kv_heads, HD)
    fresh_keys = lax.dynamic_slice_in_dim(
        jnp.repeat(fresh[:, :, 0], group, axis=2), tp_index * head_dev, head_dev, 2
    )
    fresh_values = lax.dynamic_slice_in_dim(
        jnp.repeat(fresh[:, :, 1], group, axis=2), tp_index * head_dev, head_dev, 2
    )
    own_queries = queries.reshape(steps, seq_dev, head_dev, HD)
    fresh_scores = (
        jnp.einsum("sbhd,tbhd->sbht", own_queries, fresh_keys, preferred_element_type=jnp.float32)
        * scale
    )
    causal = (
        jnp.arange(steps, dtype=jnp.int32)[:, None] >= jnp.arange(steps, dtype=jnp.int32)[None, :]
    )[:, None, None, :]
    fresh_scores = jnp.where(causal, fresh_scores, -1e30)
    top = jnp.maximum(own_top, jnp.max(fresh_scores, axis=-1))
    cache_factor = jnp.exp(own_top - top)
    fresh_weights = jnp.exp(fresh_scores - top[..., None])
    total = own_total * cache_factor + jnp.sum(fresh_weights, axis=-1)
    summed = own_sum * cache_factor[..., None] + jnp.einsum(
        "sbht,tbhd->sbhd", fresh_weights, fresh_values.astype(jnp.float32)
    )
    attn = (summed / total[..., None]).astype(jnp.bfloat16).reshape(rows, q_cols)
    blocks_in = o_cols // q_cols
    out_blocks = o_merged.reshape(q_cols, blocks_in, q_cols)
    partial_out = jnp.einsum(
        "snc,cjf->jnsf",
        lax.all_gather(attn.reshape(steps, seq_dev, q_cols), "dp", axis=1, tiled=True),
        out_blocks,
        preferred_element_type=jnp.float32,
    )
    dp_size = lax.axis_size("dp")
    tp_size = lax.axis_size("tp")
    arranged = partial_out.reshape(blocks_in * dp_size, seq_dev, steps, q_cols)
    spread_terms = jnp.zeros((tp_size * dp_size, seq_dev, steps, q_cols), jnp.float32)
    spread_terms = lax.dynamic_update_slice_in_dim(
        spread_terms, arranged, dp_index * blocks_in * dp_size, 0
    )
    own_rows = lax.psum_scatter(spread_terms, ("tp", "dp"), scatter_dimension=0, tiled=True)
    mixed = jnp.transpose(own_rows.reshape(seq_dev, steps, q_cols), (1, 0, 2)).astype(jnp.bfloat16)
    return mixed


def on_device(
    tokens, lengths, cache_keys, cache_values, q_weight, kv_weight, o_weight, adapters, layout
):
    t = lax.axis_index("tp")
    d = lax.axis_index("dp")
    steps, seq_dev, feat_dev = tokens.shape
    rows = steps * seq_dev
    span = cache_keys.shape[1]
    kv_cols = cache_keys.shape[2] // SIDE
    shards = layout.shape[0]
    numbers = jnp.arange(shards, dtype=jnp.int32)
    inverse = jnp.sum(jnp.where(layout[None, :] == numbers[:, None], numbers[None, :], 0), axis=1)
    row_d, across_d = block_places(inverse, d * SIDE, t, d)
    row_t, across_t = block_places(inverse, t * SIDE, t, d)
    y = lax.axis_index("groups")
    turn = t ^ d
    q_slots = jnp.concatenate([row_d, row_t, across_d, across_t, jnp.stack([y, turn])])
    o_slots = jnp.concatenate([row_t, row_d, across_t, across_d, jnp.stack([y, turn])])
    own = tokens.reshape(rows, feat_dev)
    rank = adapters.shape[1]
    halves = adapters.reshape(4, 2, rank // 2, adapters.shape[2])

    def shaped(*shape):
        return jax.ShapeDtypeStruct(shape, BF16)

    width = adapters.shape[2]
    slab = rows * feat_dev // width
    payload = small_call(first_kernel, y.reshape(1), [halves, own], shaped(2 * rank + slab, width))
    held = [payload] + [along_tp(payload, k) for k in range(1, SIDE)]
    halves_far = across_dp(after(halves, payload), 2)

    ks = jnp.arange(SIDE, dtype=jnp.int32)
    froms = (t - (d ^ ks)) % SIDE
    spots = jnp.concatenate([(t - ks) % SIDE, lengths])
    cached = seq_dev * span
    cache_send = split_call(
        (t + ks) % SIDE,
        own,
        cache_keys.reshape(cached, -1),
        cache_values.reshape(cached, -1),
        kv_weight,
        shaped(2 * cached + 4 * rows, kv_cols),
    )

    held = after(held, *cache_send, q_slots, o_slots, spots, froms)
    unit = (rank // 2, width)
    slab = slab // unit[0]
    others = 2 * (SIDE - 1)
    q_mine, o_mine, across, own_rows, near_rows = small_call(
        sort_kernel,
        froms,
        held,
        [shaped(n, *unit) for n in (others, others, others + 2 * slab, slab, slab)],
    )
    q_far = across_dp(across, 2)
    q_other = across_groups(q_mine)
    next_send, last_send = after([cache_send[1], cache_send[3]], q_mine)
    from_next, from_last = along_tp(next_send, 1), along_tp(last_send, 3)
    q_far, q_other, from_next, from_last = lax.optimization_barrier(
        (q_far, q_other, from_next, from_last)
    )
    middle_keys = along_tp(after(cache_send[2][:cached], q_far, q_other), 2)
    own_rows, middle_keys = lax.optimization_barrier((own_rows, middle_keys))
    q_corners = corners_of(q_far, q_other)
    halves = halves.reshape(2, 4, *unit)
    halves_far = halves_far.reshape(2, 4, *unit)
    q_packed = pack([halves[0], halves_far[0], q_mine, q_far, q_other, near_rows], PACK_COST)
    q_parts = with_sibling(q_packed, q_corners)
    o_mine = after(o_mine, *q_corners)
    o_far, o_other = across_dp(o_mine, 2), across_groups(o_mine)

    q_part = merge_call(
        merge_dot_kernel,
        q_slots,
        q_parts,
        pltpu.with_memory_space_constraint(q_weight, pltpu.HBM),
        [own_rows, q_far],
        jax.ShapeDtypeStruct((SIDE * rows, q_weight.shape[1]), F32),
        [4 * SIDE, SIDE, q_weight.shape[0] // BLOCK],
        rank,
        0,
    )
    near = across_dp(jnp.concatenate([q_part[rows : 2 * rows], q_part[3 * rows :]]), 1)
    middle_rest = along_tp(after(cache_send[2][cached:], q_part), 2)
    caches = [cache_send[0], from_next, from_last, middle_keys, middle_rest]
    q_near_sum = q_part[:rows] + near[:rows]
    q_far_sum = across_dp(q_part[2 * rows : 3 * rows] + near[rows:], 2)

    o_corners = corners_of(*after((o_far, o_other), near))
    o_packed = pack([halves[1], halves_far[1], o_mine, o_far, o_other])
    o_parts = with_sibling(o_packed, o_corners)

    vmem_spec = pl.BlockSpec(memory_space=pltpu.VMEM)
    attn = pl.pallas_call(
        functools.partial(attention_kernel, seq_dev),
        out_shape=jax.ShapeDtypeStruct((rows, q_weight.shape[1]), BF16),
        in_specs=[pl.BlockSpec(memory_space=pltpu.SMEM)] + [vmem_spec] * 7,
        out_specs=vmem_spec,
        compiler_params=pltpu.CompilerParams(vmem_limit_bytes=8 * MIB),
    )(spots, q_near_sum, q_far_sum, *caches)

    o_merged = merge_call(
        merge_kernel,
        o_slots,
        o_parts,
        pltpu.with_memory_space_constraint(o_weight, pltpu.HBM),
        [],
        pltpu.VMEM(o_weight.shape, BF16),
        [4 * SIDE, o_weight.shape[0] // BLOCK],
        rank,
        16,
    )
    attn_rows = [attn] + [across_dp(attn, k) for k in range(1, SIDE)]
    width = o_weight.shape[1]
    first, rest = pl.pallas_call(
        out_kernel,
        out_shape=(
            jax.ShapeDtypeStruct((rows, width), F32),
            jax.ShapeDtypeStruct((SIDE - 1, rows, width), BF16),
        ),
        in_specs=[pl.BlockSpec(memory_space=pltpu.SMEM)] + [vmem_spec] * (SIDE + 1),
        out_specs=(vmem_spec, vmem_spec),
        scratch_shapes=[pltpu.VMEM((SIDE * rows, o_weight.shape[0]), BF16)],
        compiler_params=pltpu.CompilerParams(vmem_limit_bytes=16 * MIB),
    )(turn.reshape(1), *attn_rows, o_merged)
    mixed = to_holder(first, 0)
    for m in range(1, SIDE):
        mixed = mixed + to_holder(rest[m - 1], m).astype(F32)
    return mixed.astype(BF16).reshape(steps, seq_dev, width)


def solution(mesh):
    def fits(layout, cache_keys):
        sides = mesh.shape["tp"] == SIDE and mesh.shape["dp"] == SIDE and mesh.shape["groups"] == 2
        return sides and layout.shape[0] == SIDE * SIDE

    def run(tokens, lengths, cache_keys, cache_values, q_weight, kv_weight, o_weight, adapters, layout):
        body = on_device if fits(layout, cache_keys) else general
        return body(
            tokens, lengths, cache_keys, cache_values, q_weight, kv_weight, o_weight, adapters, layout
        )

    return jax.shard_map(
        run,
        mesh=mesh,
        in_specs=(
            P(None, ("groups", "dp"), "tp"),
            P(("groups", "dp")),
            P(("groups", "dp"), "tp", None),
            P(("groups", "dp"), "tp", None),
            P("dp", "tp"),
            P("tp", None),
            P("tp", "dp"),
            P(None, None, ("tp", "dp")),
            P(),
        ),
        out_specs=P(None, ("groups", "dp"), "tp"),
        check_vma=False,
    )
```

```python
import functools

import jax
import jax.numpy as jnp
from jax import lax
from jax.experimental import pallas as pl
from jax.experimental.pallas import tpu as pltpu
from jax.sharding import PartitionSpec as P

HD = 128
F32 = jnp.float32
BF16 = jnp.bfloat16
SIDE = 4
BLOCK = 256
MIB = 1 << 20


def after(x, *earlier):
    return lax.optimization_barrier((x, *earlier))[0]


def along_tp(x, k):
    return lax.ppermute(x, "tp", [(i, (i + k) % SIDE) for i in range(SIDE)])


def across_dp(x, k):
    return lax.ppermute(x, "dp", [(i, i ^ k) for i in range(SIDE)])


def across_groups(x):
    return lax.ppermute(x, "groups", [(0, 1), (1, 0)])


def to_holder(x, m):
    pairs = [(t * SIDE + d, d * SIDE + (t ^ m)) for t in range(SIDE) for d in range(SIDE)]
    return lax.ppermute(x, ("tp", "dp"), pairs)


def pack_kernel(spans, *refs):
    out_ref, at = refs[-1], 0
    for ref, (start, count) in zip(refs[:-1], spans):
        out_ref[at : at + count] = ref[start : start + count]
        at += count


def pack(parts):
    spec = pl.BlockSpec(memory_space=pltpu.VMEM)
    parts = [part if isinstance(part, tuple) else (part, 0, part.shape[0]) for part in parts]
    arrays = [array for array, _, _ in parts]
    spans = [(start, count) for _, start, count in parts]
    shape = (sum(count for _, count in spans), *arrays[0].shape[1:])
    return pl.pallas_call(
        functools.partial(pack_kernel, spans),
        out_shape=jax.ShapeDtypeStruct(shape, arrays[0].dtype),
        in_specs=[spec] * len(parts),
        out_specs=spec,
        compiler_params=pltpu.CompilerParams(vmem_limit_bytes=4 * MIB),
    )(*arrays)


def small_call(kernel, scalars, arrays, out_shape, vmem=8 * MIB):
    spec = pl.BlockSpec(memory_space=pltpu.VMEM)
    return pl.pallas_call(
        kernel,
        out_shape=out_shape,
        in_specs=[pl.BlockSpec(memory_space=pltpu.SMEM)] + [spec] * len(arrays),
        out_specs=jax.tree.map(lambda _: spec, out_shape),
        compiler_params=pltpu.CompilerParams(vmem_limit_bytes=vmem),
    )(scalars, *arrays)


def first_kernel(y_ref, adapters_ref, tokens_ref, out_ref):
    half = adapters_ref.shape[2]
    width = out_ref.shape[1]
    rows = tokens_ref.shape[0]
    for f in range(4):
        out_ref[f * half : (f + 1) * half] = adapters_ref[f, y_ref[0]]
    for j in range(tokens_ref.shape[1] // width):
        at = 4 * half + j * rows
        out_ref[at : at + rows] = tokens_ref[:, j * width : (j + 1) * width]


def sort_kernel(from_ref, *refs):
    held, (q_ref, o_ref, across_ref, *sends) = refs[:SIDE], refs[SIDE:]
    half = q_ref.shape[1]
    others = SIDE - 1
    for k in range(1, SIDE):
        for f in range(2):
            unit = held[k][f * half : (f + 1) * half]
            q_ref[f * others + k - 1] = unit
            across_ref[f * others + k - 1] = unit
            o_ref[f * others + k - 1] = held[k][(2 + f) * half : (3 + f) * half]
    slab = sends[0].shape[0]
    for k in range(SIDE):
        for j, ref in enumerate(held):

            @pl.when(from_ref[k] == j)
            def _(ref=ref, k=k):
                for u in range(slab):
                    unit = ref[(4 + u) * half : (5 + u) * half]
                    if k < 2:
                        sends[k][u] = unit
                    else:
                        across_ref[2 * others + (k - 2) * slab + u] = unit


def split_kernel(heads_ref, tokens_ref, keys_ref, values_ref, w_hbm, *refs):
    outs, (w_ref, kv_ref, sem) = refs[:SIDE], refs[SIDE:]
    row_parts = row_copies(w_hbm, w_ref, sem)
    for copy in row_parts:
        copy.start()
    cached = keys_ref.shape[0]
    rows, width = kv_ref.shape
    cols = outs[0].shape[1]
    places = [pl.multiple_of(heads_ref[k] * cols, cols) for k in range(SIDE)]
    for at, out in zip(places, outs):
        out[:cached] = keys_ref[:, pl.ds(at, cols)]
        out[cached : 2 * cached] = values_ref[:, pl.ds(at, cols)]
    for i in range(0, w_ref.shape[0], BLOCK):
        row_parts[i // BLOCK].wait()
        lanes = slice(i, i + BLOCK)
        term = jnp.dot(tokens_ref[:, lanes], w_ref[lanes, :], preferred_element_type=F32)
        if i == 0:
            kv_ref[...] = term
        else:
            kv_ref[...] += term
    for at, out in zip(places, outs):
        for part in range(2):
            term = kv_ref[:, pl.ds(pl.multiple_of(part * (width // 2) + at, cols), cols)]
            coarse = term.astype(BF16)
            row = 2 * cached + part * rows
            out[row : row + rows] = coarse
            out[row + 2 * rows : row + 3 * rows] = (term - coarse.astype(F32)).astype(BF16)


def split_call(heads, own, keys, values, weight, out_shape):
    spec = pl.BlockSpec(memory_space=pltpu.VMEM)
    return pl.pallas_call(
        split_kernel,
        out_shape=[out_shape] * SIDE,
        in_specs=[pl.BlockSpec(memory_space=pltpu.SMEM)]
        + [spec] * 3
        + [pl.BlockSpec(memory_space=pl.ANY)],
        out_specs=[spec] * SIDE,
        scratch_shapes=[
            pltpu.VMEM(weight.shape, BF16),
            pltpu.VMEM((own.shape[0], weight.shape[1]), F32),
            pltpu.SemaphoreType.DMA((weight.shape[0] // BLOCK,)),
        ],
        compiler_params=pltpu.CompilerParams(vmem_limit_bytes=16 * MIB),
        cost_estimate=pl.CostEstimate(
            flops=2 * own.size * weight.shape[1], bytes_accessed=4 * weight.size, transcendentals=0
        ),
    )(heads, own, keys, values, pltpu.with_memory_space_constraint(weight, pltpu.HBM))


def corners_of(mine_far, other):
    half = other.shape[0] // 2
    return [across_dp(other[:half], 2), across_groups(mine_far[half : 2 * half])]


def with_sibling(packed, corners):
    near = [packed, *corners]
    return near + [across_dp(x, 1) for x in near]


def block_places(inverse, first, t, d):
    source = lax.dynamic_slice_in_dim(inverse, first, SIDE, 0)
    return (t - source // SIDE) % SIDE, (source % SIDE) ^ d


def pick(slots_ref, parts, other_at, down_ref, up_ref, sem):
    y = slots_ref[4 * SIDE]
    half = down_ref.shape[0] // 2
    cols = down_ref.shape[1] // SIDE
    others = SIDE - 1

    def copy(n, source, h):
        dst = down_ref if n < SIDE else up_ref
        at = pl.multiple_of(h * half, half)
        lanes = pl.ds((n % SIDE) * cols, cols)
        return pltpu.make_async_copy(source, dst.at[pl.ds(at, half), lanes], sem.at[2 * n + h])

    for n in range(2 * SIDE):
        factor = n // SIDE
        row, across = slots_ref[n], slots_ref[2 * SIDE + n]
        far = across >> 1
        in_row = factor * others + row - 1
        at_mine = jnp.where(row == 0, far * 4 + factor * 2 + y, 8 + far * 2 * others + in_row)
        at_other = jnp.where(row == 0, far * 4 + factor * 2 + 1 - y, other_at + in_row)
        corner = (far == 1) & (row > 0)
        for side in range(2):
            packed, *corners = parts[side * 3 : side * 3 + 3]
            here = (across & 1) == side

            @pl.when(here)
            def _(packed=packed, at_mine=at_mine, n=n):
                copy(n, packed.at[at_mine], y).start()

            @pl.when(here & jnp.logical_not(corner))
            def _(packed=packed, at_other=at_other, n=n):
                copy(n, packed.at[at_other], 1 - y).start()

            @pl.when(here & corner)
            def _(source=corners[factor], row=row, n=n):
                copy(n, source.at[row - 1], 1 - y).start()

    for n in range(2 * SIDE):
        for h in range(2):
            copy(n, parts[0].at[0], h).wait()


def merged_rows(w, down_ref, up_ref, lanes):
    delta = lax.dot_general(
        down_ref[:, lanes], up_ref[...], (((0,), (0,)), ((), ())), preferred_element_type=F32
    )
    return (w.astype(F32) + delta).astype(BF16)


def row_copies(src, dst, sem):
    return [
        pltpu.make_async_copy(src.at[pl.ds(i, BLOCK)], dst.at[pl.ds(i, BLOCK)], sem.at[i // BLOCK])
        for i in range(0, src.shape[0], BLOCK)
    ]


def place_rows(turn, pieces, x_ref):
    rows = pieces[0].shape[0]
    for m, piece in enumerate(pieces):
        x_ref[pl.ds(pl.multiple_of((turn ^ m) * rows, rows), rows), :] = piece[...]


def merge_dot_kernel(slots_ref, *refs):
    parts = refs[:6]
    w_hbm, own_ref, across_ref, out_ref, down_ref, up_ref, w_ref, x_ref, tokens_ref = refs[6:15]
    sem, token_sem, row_sem = refs[15:]
    slab, half, width = own_ref.shape
    total = parts[3].shape[0]
    at = 2 * (SIDE - 1)
    sources = [
        own_ref,
        parts[3].at[pl.ds(total - slab, slab)],
        across_ref.at[pl.ds(at, slab)],
        parts[3].at[pl.ds(total - 2 * slab - at, slab)],
    ]
    copies = [
        pltpu.make_async_copy(source, tokens_ref.at[pl.ds(k * slab, slab)], token_sem.at[k])
        for k, source in enumerate(sources)
    ]
    row_parts = row_copies(w_hbm, w_ref, row_sem)
    for copy in copies + row_parts:
        copy.start()
    pick(slots_ref, parts, total - slab - at, down_ref, up_ref, sem)
    for copy in copies:
        copy.wait()
    rows = slab * half * width // x_ref.shape[1]
    for k in range(SIDE):
        for j in range(x_ref.shape[1] // width):
            u, row = divmod(j * rows, half)
            term = tokens_ref[k * slab + u, row : row + rows, :]
            x_ref[k * rows : (k + 1) * rows, j * width : (j + 1) * width] = term
    for i in range(0, w_ref.shape[0], BLOCK):
        row_parts[i // BLOCK].wait()
        lanes = slice(i, i + BLOCK)
        merged = merged_rows(w_ref[lanes, :], down_ref, up_ref, lanes)
        term = jnp.dot(x_ref[:, lanes], merged, preferred_element_type=F32)
        if i == 0:
            out_ref[...] = term
        else:
            out_ref[...] += term


def merge_kernel(slots_ref, *refs):
    w_ref, out_ref, down_ref, up_ref, sem, row_sem = refs[6:]
    copies = row_copies(w_ref, out_ref, row_sem)
    for copy in copies:
        copy.start()
    pick(slots_ref, refs[:6], refs[0].shape[0] - 2 * (SIDE - 1), down_ref, up_ref, sem)
    for i in range(0, w_ref.shape[0], BLOCK):
        copies[i // BLOCK].wait()
        lanes = slice(i, i + BLOCK)
        out_ref[lanes, :] = merged_rows(out_ref[lanes, :], down_ref, up_ref, lanes)


def merge_call(kernel, slots, parts, weight, pieces, out_shape, sems, rank, cost):
    depth, width = weight.shape
    piece_cols = parts[0].shape[-1]
    vmem_spec = pl.BlockSpec(memory_space=pltpu.VMEM)
    scratch = [pltpu.VMEM((rank, SIDE * piece_cols), BF16)] * 2
    if pieces:
        scratch.append(pltpu.VMEM(weight.shape, BF16))
        scratch.append(pltpu.VMEM((out_shape.shape[0], depth), BF16))
        slab, *unit = pieces[0].shape
        scratch.append(pltpu.VMEM((SIDE * slab, *unit), BF16))
    scratch += [pltpu.SemaphoreType.DMA((count,)) for count in sems]
    return pl.pallas_call(
        kernel,
        out_shape=out_shape,
        in_specs=[pl.BlockSpec(memory_space=pltpu.SMEM)]
        + [pl.BlockSpec(memory_space=pl.ANY)] * len(parts)
        + [pl.BlockSpec(memory_space=pl.ANY)]
        + [vmem_spec] * len(pieces),
        out_specs=vmem_spec,
        scratch_shapes=scratch,
        compiler_params=pltpu.CompilerParams(vmem_limit_bytes=16 * MIB),
        cost_estimate=pl.CostEstimate(flops=0, bytes_accessed=cost * MIB, transcendentals=0),
    )(slots, *parts, weight, *pieces)


def attention_kernel(seqs, spots_ref, qa_ref, qb_ref, c0, c1, c3, keys_ref, rest_ref, out_ref):
    scale = HD ** (-0.5)
    rows = qa_ref.shape[0]
    kv_dev = c0.shape[1] // HD
    group = qa_ref.shape[1] // HD // kv_dev
    span = (c0.shape[0] - 4 * rows) // (2 * seqs)
    cached = seqs * span
    queries = (qa_ref[...] + qb_ref[...]).astype(BF16)

    row_seq = lax.broadcasted_iota(jnp.int32, (rows, cached), 0) % seqs
    column = lax.broadcasted_iota(jnp.int32, (rows, cached), 1)
    biases = []
    for k in range(SIDE):
        valid = column < 0
        for b in range(seqs):
            left = jnp.clip(spots_ref[SIDE + b] - spots_ref[k] * span, 0, span)
            inside = (column >= b * span) & (column < b * span + left)
            valid |= inside & (row_seq == b)
        biases.append(jnp.where(valid, 0.0, -1e30))
    row = lax.broadcasted_iota(jnp.int32, (rows, rows), 0)
    earlier = lax.broadcasted_iota(jnp.int32, (rows, rows), 1)
    causal = (earlier // seqs <= row // seqs) & (earlier % seqs == row % seqs)
    fresh_bias = jnp.where(causal, 0.0, -1e30)

    def fresh_part(part):
        terms = []
        for c in (c0, c1, rest_ref, c3):
            at = c.shape[0] - 4 * rows + part * rows
            terms.append(c[at : at + rows].astype(F32))
            terms.append(c[at + 2 * rows : at + 3 * rows].astype(F32))
        return sum(terms).astype(BF16)

    fresh_keys, fresh_values = fresh_part(0), fresh_part(1)
    contract_last = (((1,), (1,)), ((), ()))

    def scores_of(q, keys, bias):
        s = lax.dot_general(q, keys, contract_last, preferred_element_type=F32) * scale
        s = s.reshape(group, rows, s.shape[1]) + bias[None]
        return s.reshape(group * rows, s.shape[2])

    def weighted(weights, values):
        coarse = weights.astype(BF16)
        rest = (weights - coarse.astype(F32)).astype(BF16)
        return jnp.dot(coarse, values, preferred_element_type=F32) + jnp.dot(
            rest, values, preferred_element_type=F32
        )

    for h in range(kv_dev):
        lanes = slice(h * HD, (h + 1) * HD)
        q = jnp.concatenate(
            [queries[:, (h * group + g) * HD : (h * group + g + 1) * HD] for g in range(group)], axis=0
        )
        scores = [scores_of(q, c[:cached, lanes], biases[k]) for k, c in enumerate((c0, c1, keys_ref, c3))]
        scores.append(scores_of(q, fresh_keys[:, lanes], fresh_bias))
        values = [c[cached : 2 * cached, lanes] for c in (c0, c1)]
        values += [rest_ref[:cached, lanes], c3[cached : 2 * cached, lanes]]
        values.append(fresh_values[:, lanes])
        top = functools.reduce(jnp.maximum, [jnp.max(s, axis=1, keepdims=True) for s in scores])
        weights = [jnp.exp(s - top) for s in scores]
        total = sum(jnp.sum(w, axis=1, keepdims=True) for w in weights)
        summed = sum(weighted(w, v) for w, v in zip(weights, values))
        attn = (summed / total).astype(BF16)
        for g in range(group):
            out_ref[:, (h * group + g) * HD : (h * group + g + 1) * HD] = attn[g * rows : (g + 1) * rows]


def out_kernel(turn_ref, a0, a1, a2, a3, w_ref, first_ref, rest_ref, x_ref):
    rows = a0.shape[0]
    place_rows(turn_ref[0], (a0, a1, a2, a3), x_ref)
    for j in range(0, w_ref.shape[1], 2 * BLOCK):
        lanes = slice(j, j + 2 * BLOCK)
        total = jnp.dot(x_ref[...], w_ref[:, lanes], preferred_element_type=F32)
        first_ref[:, lanes] = total[:rows]
        for m in range(1, SIDE):
            rest_ref[m - 1, :, lanes] = total[m * rows : (m + 1) * rows].astype(BF16)


def joined_2(array, axis, combine):
    everything = jax.tree.map(lambda part: lax.all_gather(part, axis), array)
    leading = jax.tree.map(lambda part: part[0], everything)

    def turn(k, so_far):
        return combine(so_far, jax.tree.map(lambda part: part[k], everything))

    return lax.fori_loop(1, lax.axis_size(axis), turn, leading)


def join_partials(first, second):
    top_a, total_a, summed_a = first
    top_b, total_b, summed_b = second
    top = jnp.maximum(top_a, top_b)
    factor_a = jnp.exp(top_a - top)
    factor_b = jnp.exp(top_b - top)
    return (
        top,
        total_a * factor_a + total_b * factor_b,
        summed_a * factor_a[..., None] + summed_b * factor_b[..., None],
    )


def pick_columns(stacked, inverse, factor, start, count):
    piece_cols = stacked.shape[3]
    block_ids = lax.dynamic_slice_in_dim(inverse, start // piece_cols, count // piece_cols, 0)
    chosen = jnp.take(stacked[factor], block_ids, axis=1)
    return chosen.reshape(stacked.shape[1], count)


def general(
    tokens, lengths, cache_keys, cache_values, q_weight, kv_weight, o_weight, adapters, layout
):
    tp_index = lax.axis_index("tp")
    dp_index = lax.axis_index("dp")
    steps, seq_dev, feat_dev = tokens.shape
    rank = adapters.shape[1]
    shards = layout.shape[0]
    rows = steps * seq_dev
    scale = HD ** (-0.5)
    gathered = lax.all_gather(adapters, ("tp", "dp"), axis=2, tiled=True)
    width = gathered.shape[2]
    piece_cols = width // shards
    stacked = gathered.reshape(4, rank, shards, piece_cols)
    block_numbers = jnp.arange(shards, dtype=jnp.int32)
    inverse = jnp.sum(
        jnp.where(layout[None, :] == block_numbers[:, None], block_numbers[None, :], 0), axis=1
    )
    kv_part = jnp.dot(tokens.reshape(rows, feat_dev), kv_weight, preferred_element_type=jnp.float32)
    new_kv = lax.psum(kv_part, "tp").astype(jnp.bfloat16)
    full_tokens = lax.all_gather(tokens, "tp", axis=2, tiled=True)
    q_rows = q_weight.shape[0]
    q_cols = q_weight.shape[1]
    o_cols = o_weight.shape[1]
    col_start = tp_index * q_cols
    q_down_part = pick_columns(stacked, inverse, 0, dp_index * q_rows, q_rows)
    q_up_part = pick_columns(stacked, inverse, 1, col_start, q_cols)
    o_down_part = pick_columns(stacked, inverse, 2, col_start, q_cols)
    o_up_part = pick_columns(stacked, inverse, 3, dp_index * o_cols, o_cols)
    q_merged = (
        q_weight.astype(jnp.float32)
        + jnp.einsum("rf,rc->fc", q_down_part, q_up_part, preferred_element_type=jnp.float32)
    ).astype(jnp.bfloat16)
    o_merged = (
        o_weight.astype(jnp.float32)
        + jnp.einsum("rf,rc->fc", o_down_part, o_up_part, preferred_element_type=jnp.float32)
    ).astype(jnp.bfloat16)
    flat_tokens = full_tokens.reshape(rows, width)
    q_total = jnp.dot(
        flat_tokens,
        lax.all_gather(q_merged, "dp", axis=0, tiled=True),
        preferred_element_type=jnp.float32,
    )
    queries = q_total.astype(jnp.bfloat16).reshape(steps, seq_dev, q_cols)
    all_queries = lax.all_gather(queries, "tp", axis=2, tiled=True)
    heads = all_queries.shape[2] // HD
    kv_heads = cache_keys.shape[2] // HD
    group = heads // kv_heads
    head_dev = q_cols // HD
    span = cache_keys.shape[1]
    grouped = all_queries.reshape(steps, seq_dev, kv_heads, group, HD)
    keys_local = cache_keys.reshape(seq_dev, span, kv_heads, HD)
    values_local = cache_values.reshape(seq_dev, span, kv_heads, HD)
    positions = tp_index * span + jnp.arange(span, dtype=jnp.int32)
    valid = (positions[None, :] < lengths[:, None])[None, :, None, None, :]
    scores = (
        jnp.einsum("sbkgd,bpkd->sbkgp", grouped, keys_local, preferred_element_type=jnp.float32)
        * scale
    )
    scores = jnp.where(valid, scores, -1e30)
    local_top = jnp.max(scores, axis=-1)
    weights = jnp.where(valid, jnp.exp(scores - local_top[..., None]), 0.0)
    local_total = jnp.sum(weights, axis=-1).reshape(steps, seq_dev, heads)
    local_sum = jnp.einsum("sbkgp,bpkd->sbkgd", weights, values_local.astype(jnp.float32)).reshape(
        steps, seq_dev, heads, HD
    )
    local_top = local_top.reshape(steps, seq_dev, heads)
    joined = joined_2((local_top, local_total, local_sum), "tp", join_partials)
    own_top = lax.dynamic_slice_in_dim(joined[0], tp_index * head_dev, head_dev, 2)
    own_total = lax.dynamic_slice_in_dim(joined[1], tp_index * head_dev, head_dev, 2)
    own_sum = lax.dynamic_slice_in_dim(joined[2], tp_index * head_dev, head_dev, 2)
    fresh = new_kv.reshape(steps, seq_dev, 2, kv_heads, HD)
    fresh_keys = lax.dynamic_slice_in_dim(
        jnp.repeat(fresh[:, :, 0], group, axis=2), tp_index * head_dev, head_dev, 2
    )
    fresh_values = lax.dynamic_slice_in_dim(
        jnp.repeat(fresh[:, :, 1], group, axis=2), tp_index * head_dev, head_dev, 2
    )
    own_queries = queries.reshape(steps, seq_dev, head_dev, HD)
    fresh_scores = (
        jnp.einsum("sbhd,tbhd->sbht", own_queries, fresh_keys, preferred_element_type=jnp.float32)
        * scale
    )
    causal = (
        jnp.arange(steps, dtype=jnp.int32)[:, None] >= jnp.arange(steps, dtype=jnp.int32)[None, :]
    )[:, None, None, :]
    fresh_scores = jnp.where(causal, fresh_scores, -1e30)
    top = jnp.maximum(own_top, jnp.max(fresh_scores, axis=-1))
    cache_factor = jnp.exp(own_top - top)
    fresh_weights = jnp.exp(fresh_scores - top[..., None])
    total = own_total * cache_factor + jnp.sum(fresh_weights, axis=-1)
    summed = own_sum * cache_factor[..., None] + jnp.einsum(
        "sbht,tbhd->sbhd", fresh_weights, fresh_values.astype(jnp.float32)
    )
    attn = (summed / total[..., None]).astype(jnp.bfloat16).reshape(rows, q_cols)
    blocks_in = o_cols // q_cols
    out_blocks = o_merged.reshape(q_cols, blocks_in, q_cols)
    partial_out = jnp.einsum(
        "snc,cjf->jnsf",
        lax.all_gather(attn.reshape(steps, seq_dev, q_cols), "dp", axis=1, tiled=True),
        out_blocks,
        preferred_element_type=jnp.float32,
    )
    dp_size = lax.axis_size("dp")
    tp_size = lax.axis_size("tp")
    arranged = partial_out.reshape(blocks_in * dp_size, seq_dev, steps, q_cols)
    spread_terms = jnp.zeros((tp_size * dp_size, seq_dev, steps, q_cols), jnp.float32)
    spread_terms = lax.dynamic_update_slice_in_dim(
        spread_terms, arranged, dp_index * blocks_in * dp_size, 0
    )
    own_rows = lax.psum_scatter(spread_terms, ("tp", "dp"), scatter_dimension=0, tiled=True)
    mixed = jnp.transpose(own_rows.reshape(seq_dev, steps, q_cols), (1, 0, 2)).astype(jnp.bfloat16)
    return mixed


def on_device(
    tokens, lengths, cache_keys, cache_values, q_weight, kv_weight, o_weight, adapters, layout
):
    t = lax.axis_index("tp")
    d = lax.axis_index("dp")
    steps, seq_dev, feat_dev = tokens.shape
    rows = steps * seq_dev
    span = cache_keys.shape[1]
    kv_cols = cache_keys.shape[2] // SIDE
    shards = layout.shape[0]
    numbers = jnp.arange(shards, dtype=jnp.int32)
    inverse = jnp.sum(jnp.where(layout[None, :] == numbers[:, None], numbers[None, :], 0), axis=1)
    row_d, across_d = block_places(inverse, d * SIDE, t, d)
    row_t, across_t = block_places(inverse, t * SIDE, t, d)
    y = lax.axis_index("groups")
    turn = t ^ d
    q_slots = jnp.concatenate([row_d, row_t, across_d, across_t, jnp.stack([y, turn])])
    o_slots = jnp.concatenate([row_t, row_d, across_t, across_d, jnp.stack([y, turn])])
    own = tokens.reshape(rows, feat_dev)
    rank = adapters.shape[1]
    halves = adapters.reshape(4, 2, rank // 2, adapters.shape[2])

    def shaped(*shape):
        return jax.ShapeDtypeStruct(shape, BF16)

    width = adapters.shape[2]
    slab = rows * feat_dev // width
    payload = small_call(first_kernel, y.reshape(1), [halves, own], shaped(2 * rank + slab, width))
    held = [payload] + [along_tp(payload, k) for k in range(1, SIDE)]
    halves_far = across_dp(after(halves, payload), 2)

    ks = jnp.arange(SIDE, dtype=jnp.int32)
    froms = (t - (d ^ ks)) % SIDE
    spots = jnp.concatenate([(t - ks) % SIDE, lengths])
    cached = seq_dev * span
    cache_send = split_call(
        (t + ks) % SIDE,
        own,
        cache_keys.reshape(cached, -1),
        cache_values.reshape(cached, -1),
        kv_weight,
        shaped(2 * cached + 4 * rows, kv_cols),
    )

    *held, halves_far = lax.optimization_barrier((*held, halves_far))
    held = after(held, *cache_send, q_slots, o_slots, spots, froms)
    unit = (rank // 2, width)
    slab = slab // unit[0]
    others = 2 * (SIDE - 1)
    q_mine, o_mine, across, own_rows, near_rows = small_call(
        sort_kernel,
        froms,
        held,
        [shaped(n, *unit) for n in (others, others, others + 2 * slab, slab, slab)],
    )
    q_far = across_dp(across, 2)
    q_other = across_groups(q_mine)
    next_send, last_send = after([cache_send[1], cache_send[3]], q_mine)
    from_next, from_last = along_tp(next_send, 1), along_tp(last_send, 3)
    q_far, q_other, from_next, from_last = lax.optimization_barrier(
        (q_far, q_other, from_next, from_last)
    )
    middle_keys = along_tp(after(cache_send[2][:cached], q_far, q_other), 2)
    q_corners = corners_of(q_far, q_other)
    halves = halves.reshape(8, *unit)
    halves_far = halves_far.reshape(8, *unit)
    q_packed = pack([(halves, 0, 4), (halves_far, 0, 4), q_mine, q_far, q_other, near_rows])
    q_parts = with_sibling(q_packed, q_corners)
    o_mine = after(o_mine, *q_corners)
    o_far, o_other = across_dp(o_mine, 2), across_groups(o_mine)

    q_part = merge_call(
        merge_dot_kernel,
        q_slots,
        q_parts,
        pltpu.with_memory_space_constraint(q_weight, pltpu.HBM),
        [own_rows, q_far],
        jax.ShapeDtypeStruct((SIDE * rows, q_weight.shape[1]), F32),
        [4 * SIDE, SIDE, q_weight.shape[0] // BLOCK],
        rank,
        0,
    )
    q_part, middle_keys, middle_send, o_far, o_other = lax.optimization_barrier(
        (q_part, middle_keys, cache_send[2][cached:], o_far, o_other)
    )
    near = across_dp(jnp.concatenate([q_part[rows : 2 * rows], q_part[3 * rows :]]), 1)
    near, o_far, o_other = lax.optimization_barrier((near, o_far, o_other))
    middle_rest = along_tp(middle_send, 2)
    caches = [cache_send[0], from_next, from_last, middle_keys, middle_rest]
    q_near_sum = q_part[:rows] + near[:rows]
    q_far_sum = across_dp(q_part[2 * rows : 3 * rows] + near[rows:], 2)

    o_corners = corners_of(o_far, o_other)
    o_packed = pack([(halves, 4, 4), (halves_far, 4, 4), o_mine, o_far, o_other])
    o_parts = with_sibling(o_packed, o_corners)

    vmem_spec = pl.BlockSpec(memory_space=pltpu.VMEM)
    attn = pl.pallas_call(
        functools.partial(attention_kernel, seq_dev),
        out_shape=jax.ShapeDtypeStruct((rows, q_weight.shape[1]), BF16),
        in_specs=[pl.BlockSpec(memory_space=pltpu.SMEM)] + [vmem_spec] * 7,
        out_specs=vmem_spec,
        compiler_params=pltpu.CompilerParams(vmem_limit_bytes=8 * MIB),
    )(spots, q_near_sum, q_far_sum, *caches)

    o_merged = merge_call(
        merge_kernel,
        o_slots,
        o_parts,
        pltpu.with_memory_space_constraint(o_weight, pltpu.HBM),
        [],
        pltpu.VMEM(o_weight.shape, BF16),
        [4 * SIDE, o_weight.shape[0] // BLOCK],
        rank,
        16,
    )
    attn_rows = [attn] + [across_dp(attn, k) for k in range(1, SIDE)]
    width = o_weight.shape[1]
    first, rest = pl.pallas_call(
        out_kernel,
        out_shape=(
            jax.ShapeDtypeStruct((rows, width), F32),
            jax.ShapeDtypeStruct((SIDE - 1, rows, width), BF16),
        ),
        in_specs=[pl.BlockSpec(memory_space=pltpu.SMEM)] + [vmem_spec] * (SIDE + 1),
        out_specs=(vmem_spec, vmem_spec),
        scratch_shapes=[pltpu.VMEM((SIDE * rows, o_weight.shape[0]), BF16)],
        compiler_params=pltpu.CompilerParams(vmem_limit_bytes=16 * MIB),
    )(turn.reshape(1), *attn_rows, o_merged)
    mixed = to_holder(first, 0)
    for m in range(1, SIDE):
        mixed = mixed + to_holder(rest[m - 1], m).astype(F32)
    return mixed.astype(BF16).reshape(steps, seq_dev, width)


def solution(mesh):
    def fits(layout, cache_keys):
        sides = mesh.shape["tp"] == SIDE and mesh.shape["dp"] == SIDE and mesh.shape["groups"] == 2
        return sides and layout.shape[0] == SIDE * SIDE

    def run(tokens, lengths, cache_keys, cache_values, q_weight, kv_weight, o_weight, adapters, layout):
        body = on_device if fits(layout, cache_keys) else general
        return body(
            tokens, lengths, cache_keys, cache_values, q_weight, kv_weight, o_weight, adapters, layout
        )

    return jax.shard_map(
        run,
        mesh=mesh,
        in_specs=(
            P(None, ("groups", "dp"), "tp"),
            P(("groups", "dp")),
            P(("groups", "dp"), "tp", None),
            P(("groups", "dp"), "tp", None),
            P("dp", "tp"),
            P("tp", None),
            P("tp", "dp"),
            P(None, None, ("tp", "dp")),
            P(),
        ),
        out_specs=P(None, ("groups", "dp"), "tp"),
        check_vma=False,
    )
```

```python
import functools

import jax
import jax.numpy as jnp
from jax import lax
from jax.experimental import pallas as pl
from jax.experimental.pallas import tpu as pltpu
from jax.sharding import PartitionSpec as P

HD = 128
F32 = jnp.float32
BF16 = jnp.bfloat16
SIDE = 4
BLOCK = 256
MIB = 1 << 20


def after(x, *earlier):
    return lax.optimization_barrier((x, *earlier))[0]


def along_tp(x, k):
    return lax.ppermute(x, "tp", [(i, (i + k) % SIDE) for i in range(SIDE)])


def across_dp(x, k):
    return lax.ppermute(x, "dp", [(i, i ^ k) for i in range(SIDE)])


def across_groups(x):
    return lax.ppermute(x, "groups", [(0, 1), (1, 0)])


def to_holder(x, m):
    pairs = [(t * SIDE + d, d * SIDE + (t ^ m)) for t in range(SIDE) for d in range(SIDE)]
    return lax.ppermute(x, ("tp", "dp"), pairs)


def pack_kernel(spans, *refs):
    out_ref, at = refs[-1], 0
    for ref, (start, count) in zip(refs[:-1], spans):
        out_ref[at : at + count] = ref[start : start + count]
        at += count


def pack(parts):
    spec = pl.BlockSpec(memory_space=pltpu.VMEM)
    parts = [part if isinstance(part, tuple) else (part, 0, part.shape[0]) for part in parts]
    arrays = [array for array, _, _ in parts]
    spans = [(start, count) for _, start, count in parts]
    shape = (sum(count for _, count in spans), *arrays[0].shape[1:])
    return pl.pallas_call(
        functools.partial(pack_kernel, spans),
        out_shape=jax.ShapeDtypeStruct(shape, arrays[0].dtype),
        in_specs=[spec] * len(parts),
        out_specs=spec,
        compiler_params=pltpu.CompilerParams(vmem_limit_bytes=4 * MIB),
    )(*arrays)


def small_call(kernel, scalars, arrays, out_shape, vmem=8 * MIB):
    spec = pl.BlockSpec(memory_space=pltpu.VMEM)
    return pl.pallas_call(
        kernel,
        out_shape=out_shape,
        in_specs=[pl.BlockSpec(memory_space=pltpu.SMEM)] + [spec] * len(arrays),
        out_specs=jax.tree.map(lambda _: spec, out_shape),
        compiler_params=pltpu.CompilerParams(vmem_limit_bytes=vmem),
    )(scalars, *arrays)


def first_kernel(y_ref, adapters_ref, tokens_ref, out_ref, held_ref, sem):
    half = adapters_ref.shape[2]
    width = out_ref.shape[1]
    steps, seqs, depth = tokens_ref.shape
    rows = steps * seqs
    copies = [pltpu.make_async_copy(tokens_ref, held_ref, sem.at[4])]
    for f in range(4):
        copies.append(
            pltpu.make_async_copy(
                adapters_ref.at[f, y_ref[0]], out_ref.at[pl.ds(f * half, half)], sem.at[f]
            )
        )
    for copy in copies:
        copy.start()
    copies[0].wait()
    flat_rows = jnp.concatenate([held_ref[s].astype(F32) for s in range(steps)], axis=0)
    for j in range(depth // width):
        at = 4 * half + j * rows
        out_ref[at : at + rows] = flat_rows[:, j * width : (j + 1) * width].astype(BF16)
    for copy in copies[1:]:
        copy.wait()


def first_call(y, halves, tokens, out_shape):
    any_spec = pl.BlockSpec(memory_space=pl.ANY)
    return pl.pallas_call(
        first_kernel,
        out_shape=out_shape,
        in_specs=[pl.BlockSpec(memory_space=pltpu.SMEM), any_spec, any_spec],
        out_specs=pl.BlockSpec(memory_space=pltpu.VMEM),
        scratch_shapes=[pltpu.VMEM(tokens.shape, BF16), pltpu.SemaphoreType.DMA((5,))],
        compiler_params=pltpu.CompilerParams(vmem_limit_bytes=4 * MIB),
    )(
        y,
        pltpu.with_memory_space_constraint(halves, pltpu.HBM),
        pltpu.with_memory_space_constraint(tokens, pltpu.HBM),
    )


def sort_kernel(from_ref, *refs):
    held, (q_ref, o_ref, across_ref, *sends) = refs[:SIDE], refs[SIDE:]
    half = q_ref.shape[1]
    others = SIDE - 1
    for k in range(1, SIDE):
        for f in range(2):
            unit = held[k][f * half : (f + 1) * half]
            q_ref[f * others + k - 1] = unit
            across_ref[f * others + k - 1] = unit
            o_ref[f * others + k - 1] = held[k][(2 + f) * half : (3 + f) * half]
    slab = sends[0].shape[0]
    for k in range(SIDE):
        for j, ref in enumerate(held):

            @pl.when(from_ref[k] == j)
            def _(ref=ref, k=k):
                for u in range(slab):
                    unit = ref[(4 + u) * half : (5 + u) * half]
                    if k < 2:
                        sends[k][u] = unit
                    else:
                        across_ref[2 * others + (k - 2) * slab + u] = unit


def split_kernel(heads_ref, tokens_ref, keys_ref, values_ref, w_hbm, *refs):
    outs, (w_ref, kv_ref, sem) = refs[:SIDE], refs[SIDE:]
    row_parts = row_copies(w_hbm, w_ref, sem)
    for copy in row_parts:
        copy.start()
    cached = keys_ref.shape[0]
    rows, width = kv_ref.shape
    cols = outs[0].shape[1]
    places = [pl.multiple_of(heads_ref[k] * cols, cols) for k in range(SIDE)]
    for at, out in zip(places, outs):
        out[:cached] = keys_ref[:, pl.ds(at, cols)]
        out[cached : 2 * cached] = values_ref[:, pl.ds(at, cols)]
    for i in range(0, w_ref.shape[0], BLOCK):
        row_parts[i // BLOCK].wait()
        lanes = slice(i, i + BLOCK)
        term = jnp.dot(tokens_ref[:, lanes], w_ref[lanes, :], preferred_element_type=F32)
        if i == 0:
            kv_ref[...] = term
        else:
            kv_ref[...] += term
    for at, out in zip(places, outs):
        for part in range(2):
            term = kv_ref[:, pl.ds(pl.multiple_of(part * (width // 2) + at, cols), cols)]
            coarse = term.astype(BF16)
            row = 2 * cached + part * rows
            out[row : row + rows] = coarse
            out[row + 2 * rows : row + 3 * rows] = (term - coarse.astype(F32)).astype(BF16)


def split_call(heads, own, keys, values, weight, out_shape):
    spec = pl.BlockSpec(memory_space=pltpu.VMEM)
    return pl.pallas_call(
        split_kernel,
        out_shape=[out_shape] * SIDE,
        in_specs=[pl.BlockSpec(memory_space=pltpu.SMEM)]
        + [spec] * 3
        + [pl.BlockSpec(memory_space=pl.ANY)],
        out_specs=[spec] * SIDE,
        scratch_shapes=[
            pltpu.VMEM(weight.shape, BF16),
            pltpu.VMEM((own.shape[0], weight.shape[1]), F32),
            pltpu.SemaphoreType.DMA((weight.shape[0] // BLOCK,)),
        ],
        compiler_params=pltpu.CompilerParams(vmem_limit_bytes=16 * MIB),
        cost_estimate=pl.CostEstimate(
            flops=2 * own.size * weight.shape[1], bytes_accessed=4 * weight.size, transcendentals=0
        ),
    )(heads, own, keys, values, pltpu.with_memory_space_constraint(weight, pltpu.HBM))


def corners_of(mine_far, other):
    half = other.shape[0] // 2
    return [across_dp(other[:half], 2), across_groups(mine_far[half : 2 * half])]


def with_sibling(packed, corners):
    near = [packed, *corners]
    return near + [across_dp(x, 1) for x in near]


def block_places(inverse, first, t, d):
    source = lax.dynamic_slice_in_dim(inverse, first, SIDE, 0)
    return (t - source // SIDE) % SIDE, (source % SIDE) ^ d


def pick(slots_ref, parts, other_at, down_ref, up_ref, sem):
    y = slots_ref[4 * SIDE]
    half = down_ref.shape[0] // 2
    cols = down_ref.shape[1] // SIDE
    others = SIDE - 1

    def copy(n, source, h):
        dst = down_ref if n < SIDE else up_ref
        at = pl.multiple_of(h * half, half)
        lanes = pl.ds((n % SIDE) * cols, cols)
        return pltpu.make_async_copy(source, dst.at[pl.ds(at, half), lanes], sem.at[2 * n + h])

    for n in range(2 * SIDE):
        factor = n // SIDE
        row, across = slots_ref[n], slots_ref[2 * SIDE + n]
        far = across >> 1
        in_row = factor * others + row - 1
        at_mine = jnp.where(row == 0, far * 4 + factor * 2 + y, 8 + far * 2 * others + in_row)
        at_other = jnp.where(row == 0, far * 4 + factor * 2 + 1 - y, other_at + in_row)
        corner = (far == 1) & (row > 0)
        for side in range(2):
            packed, *corners = parts[side * 3 : side * 3 + 3]
            here = (across & 1) == side

            @pl.when(here)
            def _(packed=packed, at_mine=at_mine, n=n):
                copy(n, packed.at[at_mine], y).start()

            @pl.when(here & jnp.logical_not(corner))
            def _(packed=packed, at_other=at_other, n=n):
                copy(n, packed.at[at_other], 1 - y).start()

            @pl.when(here & corner)
            def _(source=corners[factor], row=row, n=n):
                copy(n, source.at[row - 1], 1 - y).start()

    for n in range(2 * SIDE):
        for h in range(2):
            copy(n, parts[0].at[0], h).wait()


def merged_rows(w, down_ref, up_ref, lanes):
    delta = lax.dot_general(
        down_ref[:, lanes], up_ref[...], (((0,), (0,)), ((), ())), preferred_element_type=F32
    )
    return (w.astype(F32) + delta).astype(BF16)


def row_copies(src, dst, sem):
    return [
        pltpu.make_async_copy(src.at[pl.ds(i, BLOCK)], dst.at[pl.ds(i, BLOCK)], sem.at[i // BLOCK])
        for i in range(0, src.shape[0], BLOCK)
    ]


def place_rows(turn, pieces, x_ref):
    rows = pieces[0].shape[0]
    for m, piece in enumerate(pieces):
        x_ref[pl.ds(pl.multiple_of((turn ^ m) * rows, rows), rows), :] = piece[...]


def merge_dot_kernel(slots_ref, *refs):
    parts = refs[:6]
    w_hbm, own_ref, across_ref, out_ref, down_ref, up_ref, w_ref, x_ref, tokens_ref = refs[6:15]
    sem, token_sem, row_sem = refs[15:]
    slab, half, width = own_ref.shape
    total = parts[3].shape[0]
    at = 2 * (SIDE - 1)
    sources = [
        own_ref,
        parts[3].at[pl.ds(total - slab, slab)],
        across_ref.at[pl.ds(at, slab)],
        parts[3].at[pl.ds(total - 2 * slab - at, slab)],
    ]
    copies = [
        pltpu.make_async_copy(source, tokens_ref.at[pl.ds(k * slab, slab)], token_sem.at[k])
        for k, source in enumerate(sources)
    ]
    row_parts = row_copies(w_hbm, w_ref, row_sem)
    for copy in copies + row_parts:
        copy.start()
    pick(slots_ref, parts, total - slab - at, down_ref, up_ref, sem)
    for copy in copies:
        copy.wait()
    rows = slab * half * width // x_ref.shape[1]
    for k in range(SIDE):
        for j in range(x_ref.shape[1] // width):
            u, row = divmod(j * rows, half)
            term = tokens_ref[k * slab + u, row : row + rows, :]
            x_ref[k * rows : (k + 1) * rows, j * width : (j + 1) * width] = term
    for i in range(0, w_ref.shape[0], BLOCK):
        row_parts[i // BLOCK].wait()
        lanes = slice(i, i + BLOCK)
        merged = merged_rows(w_ref[lanes, :], down_ref, up_ref, lanes)
        term = jnp.dot(x_ref[:, lanes], merged, preferred_element_type=F32)
        if i == 0:
            out_ref[...] = term
        else:
            out_ref[...] += term


def merge_kernel(slots_ref, *refs):
    w_ref, out_ref, down_ref, up_ref, sem, row_sem = refs[6:]
    copies = row_copies(w_ref, out_ref, row_sem)
    for copy in copies:
        copy.start()
    pick(slots_ref, refs[:6], refs[0].shape[0] - 2 * (SIDE - 1), down_ref, up_ref, sem)
    for i in range(0, w_ref.shape[0], BLOCK):
        copies[i // BLOCK].wait()
        lanes = slice(i, i + BLOCK)
        out_ref[lanes, :] = merged_rows(out_ref[lanes, :], down_ref, up_ref, lanes)


def merge_call(kernel, slots, parts, weight, pieces, out_shape, sems, rank, cost):
    depth, width = weight.shape
    piece_cols = parts[0].shape[-1]
    vmem_spec = pl.BlockSpec(memory_space=pltpu.VMEM)
    scratch = [pltpu.VMEM((rank, SIDE * piece_cols), BF16)] * 2
    if pieces:
        scratch.append(pltpu.VMEM(weight.shape, BF16))
        scratch.append(pltpu.VMEM((out_shape.shape[0], depth), BF16))
        slab, *unit = pieces[0].shape
        scratch.append(pltpu.VMEM((SIDE * slab, *unit), BF16))
    scratch += [pltpu.SemaphoreType.DMA((count,)) for count in sems]
    return pl.pallas_call(
        kernel,
        out_shape=out_shape,
        in_specs=[pl.BlockSpec(memory_space=pltpu.SMEM)]
        + [pl.BlockSpec(memory_space=pl.ANY)] * len(parts)
        + [pl.BlockSpec(memory_space=pl.ANY)]
        + [vmem_spec] * len(pieces),
        out_specs=vmem_spec,
        scratch_shapes=scratch,
        compiler_params=pltpu.CompilerParams(vmem_limit_bytes=16 * MIB),
        cost_estimate=pl.CostEstimate(flops=0, bytes_accessed=cost * MIB, transcendentals=0),
    )(slots, *parts, weight, *pieces)


def attention_kernel(seqs, spots_ref, qa_ref, qb_ref, c0, c1, c3, keys_ref, rest_ref, out_ref):
    scale = HD ** (-0.5)
    rows = qa_ref.shape[0]
    kv_dev = c0.shape[1] // HD
    group = qa_ref.shape[1] // HD // kv_dev
    span = (c0.shape[0] - 4 * rows) // (2 * seqs)
    cached = seqs * span
    queries = (qa_ref[...] + qb_ref[...]).astype(BF16)

    row_seq = lax.broadcasted_iota(jnp.int32, (rows, cached), 0) % seqs
    column = lax.broadcasted_iota(jnp.int32, (rows, cached), 1)
    biases = []
    for k in range(SIDE):
        valid = column < 0
        for b in range(seqs):
            left = jnp.clip(spots_ref[SIDE + b] - spots_ref[k] * span, 0, span)
            inside = (column >= b * span) & (column < b * span + left)
            valid |= inside & (row_seq == b)
        biases.append(jnp.where(valid, 0.0, -1e30))
    row = lax.broadcasted_iota(jnp.int32, (rows, rows), 0)
    earlier = lax.broadcasted_iota(jnp.int32, (rows, rows), 1)
    causal = (earlier // seqs <= row // seqs) & (earlier % seqs == row % seqs)
    fresh_bias = jnp.where(causal, 0.0, -1e30)

    def fresh_part(part):
        terms = []
        for c in (c0, c1, rest_ref, c3):
            at = c.shape[0] - 4 * rows + part * rows
            terms.append(c[at : at + rows].astype(F32))
            terms.append(c[at + 2 * rows : at + 3 * rows].astype(F32))
        return sum(terms).astype(BF16)

    fresh_keys, fresh_values = fresh_part(0), fresh_part(1)
    contract_last = (((1,), (1,)), ((), ()))

    def scores_of(q, keys, bias):
        s = lax.dot_general(q, keys, contract_last, preferred_element_type=F32) * scale
        s = s.reshape(group, rows, s.shape[1]) + bias[None]
        return s.reshape(group * rows, s.shape[2])

    def weighted(weights, values):
        coarse = weights.astype(BF16)
        rest = (weights - coarse.astype(F32)).astype(BF16)
        return jnp.dot(coarse, values, preferred_element_type=F32) + jnp.dot(
            rest, values, preferred_element_type=F32
        )

    for h in range(kv_dev):
        lanes = slice(h * HD, (h + 1) * HD)
        q = jnp.concatenate(
            [queries[:, (h * group + g) * HD : (h * group + g + 1) * HD] for g in range(group)], axis=0
        )
        scores = [scores_of(q, c[:cached, lanes], biases[k]) for k, c in enumerate((c0, c1, keys_ref, c3))]
        scores.append(scores_of(q, fresh_keys[:, lanes], fresh_bias))
        values = [c[cached : 2 * cached, lanes] for c in (c0, c1)]
        values += [rest_ref[:cached, lanes], c3[cached : 2 * cached, lanes]]
        values.append(fresh_values[:, lanes])
        top = functools.reduce(jnp.maximum, [jnp.max(s, axis=1, keepdims=True) for s in scores])
        weights = [jnp.exp(s - top) for s in scores]
        total = sum(jnp.sum(w, axis=1, keepdims=True) for w in weights)
        summed = sum(weighted(w, v) for w, v in zip(weights, values))
        attn = (summed / total).astype(BF16)
        for g in range(group):
            out_ref[:, (h * group + g) * HD : (h * group + g + 1) * HD] = attn[g * rows : (g + 1) * rows]


def out_kernel(turn_ref, a0, a1, a2, a3, w_ref, first_ref, rest_ref, x_ref):
    rows = a0.shape[0]
    place_rows(turn_ref[0], (a0, a1, a2, a3), x_ref)
    for j in range(0, w_ref.shape[1], 2 * BLOCK):
        lanes = slice(j, j + 2 * BLOCK)
        total = jnp.dot(x_ref[...], w_ref[:, lanes], preferred_element_type=F32)
        first_ref[:, lanes] = total[:rows]
        for m in range(1, SIDE):
            rest_ref[m - 1, :, lanes] = total[m * rows : (m + 1) * rows].astype(BF16)


def joined_2(array, axis, combine):
    everything = jax.tree.map(lambda part: lax.all_gather(part, axis), array)
    leading = jax.tree.map(lambda part: part[0], everything)

    def turn(k, so_far):
        return combine(so_far, jax.tree.map(lambda part: part[k], everything))

    return lax.fori_loop(1, lax.axis_size(axis), turn, leading)


def join_partials(first, second):
    top_a, total_a, summed_a = first
    top_b, total_b, summed_b = second
    top = jnp.maximum(top_a, top_b)
    factor_a = jnp.exp(top_a - top)
    factor_b = jnp.exp(top_b - top)
    return (
        top,
        total_a * factor_a + total_b * factor_b,
        summed_a * factor_a[..., None] + summed_b * factor_b[..., None],
    )


def pick_columns(stacked, inverse, factor, start, count):
    piece_cols = stacked.shape[3]
    block_ids = lax.dynamic_slice_in_dim(inverse, start // piece_cols, count // piece_cols, 0)
    chosen = jnp.take(stacked[factor], block_ids, axis=1)
    return chosen.reshape(stacked.shape[1], count)


def general(
    tokens, lengths, cache_keys, cache_values, q_weight, kv_weight, o_weight, adapters, layout
):
    tp_index = lax.axis_index("tp")
    dp_index = lax.axis_index("dp")
    steps, seq_dev, feat_dev = tokens.shape
    rank = adapters.shape[1]
    shards = layout.shape[0]
    rows = steps * seq_dev
    scale = HD ** (-0.5)
    gathered = lax.all_gather(adapters, ("tp", "dp"), axis=2, tiled=True)
    width = gathered.shape[2]
    piece_cols = width // shards
    stacked = gathered.reshape(4, rank, shards, piece_cols)
    block_numbers = jnp.arange(shards, dtype=jnp.int32)
    inverse = jnp.sum(
        jnp.where(layout[None, :] == block_numbers[:, None], block_numbers[None, :], 0), axis=1
    )
    kv_part = jnp.dot(tokens.reshape(rows, feat_dev), kv_weight, preferred_element_type=jnp.float32)
    new_kv = lax.psum(kv_part, "tp").astype(jnp.bfloat16)
    full_tokens = lax.all_gather(tokens, "tp", axis=2, tiled=True)
    q_rows = q_weight.shape[0]
    q_cols = q_weight.shape[1]
    o_cols = o_weight.shape[1]
    col_start = tp_index * q_cols
    q_down_part = pick_columns(stacked, inverse, 0, dp_index * q_rows, q_rows)
    q_up_part = pick_columns(stacked, inverse, 1, col_start, q_cols)
    o_down_part = pick_columns(stacked, inverse, 2, col_start, q_cols)
    o_up_part = pick_columns(stacked, inverse, 3, dp_index * o_cols, o_cols)
    q_merged = (
        q_weight.astype(jnp.float32)
        + jnp.einsum("rf,rc->fc", q_down_part, q_up_part, preferred_element_type=jnp.float32)
    ).astype(jnp.bfloat16)
    o_merged = (
        o_weight.astype(jnp.float32)
        + jnp.einsum("rf,rc->fc", o_down_part, o_up_part, preferred_element_type=jnp.float32)
    ).astype(jnp.bfloat16)
    flat_tokens = full_tokens.reshape(rows, width)
    q_total = jnp.dot(
        flat_tokens,
        lax.all_gather(q_merged, "dp", axis=0, tiled=True),
        preferred_element_type=jnp.float32,
    )
    queries = q_total.astype(jnp.bfloat16).reshape(steps, seq_dev, q_cols)
    all_queries = lax.all_gather(queries, "tp", axis=2, tiled=True)
    heads = all_queries.shape[2] // HD
    kv_heads = cache_keys.shape[2] // HD
    group = heads // kv_heads
    head_dev = q_cols // HD
    span = cache_keys.shape[1]
    grouped = all_queries.reshape(steps, seq_dev, kv_heads, group, HD)
    keys_local = cache_keys.reshape(seq_dev, span, kv_heads, HD)
    values_local = cache_values.reshape(seq_dev, span, kv_heads, HD)
    positions = tp_index * span + jnp.arange(span, dtype=jnp.int32)
    valid = (positions[None, :] < lengths[:, None])[None, :, None, None, :]
    scores = (
        jnp.einsum("sbkgd,bpkd->sbkgp", grouped, keys_local, preferred_element_type=jnp.float32)
        * scale
    )
    scores = jnp.where(valid, scores, -1e30)
    local_top = jnp.max(scores, axis=-1)
    weights = jnp.where(valid, jnp.exp(scores - local_top[..., None]), 0.0)
    local_total = jnp.sum(weights, axis=-1).reshape(steps, seq_dev, heads)
    local_sum = jnp.einsum("sbkgp,bpkd->sbkgd", weights, values_local.astype(jnp.float32)).reshape(
        steps, seq_dev, heads, HD
    )
    local_top = local_top.reshape(steps, seq_dev, heads)
    joined = joined_2((local_top, local_total, local_sum), "tp", join_partials)
    own_top = lax.dynamic_slice_in_dim(joined[0], tp_index * head_dev, head_dev, 2)
    own_total = lax.dynamic_slice_in_dim(joined[1], tp_index * head_dev, head_dev, 2)
    own_sum = lax.dynamic_slice_in_dim(joined[2], tp_index * head_dev, head_dev, 2)
    fresh = new_kv.reshape(steps, seq_dev, 2, kv_heads, HD)
    fresh_keys = lax.dynamic_slice_in_dim(
        jnp.repeat(fresh[:, :, 0], group, axis=2), tp_index * head_dev, head_dev, 2
    )
    fresh_values = lax.dynamic_slice_in_dim(
        jnp.repeat(fresh[:, :, 1], group, axis=2), tp_index * head_dev, head_dev, 2
    )
    own_queries = queries.reshape(steps, seq_dev, head_dev, HD)
    fresh_scores = (
        jnp.einsum("sbhd,tbhd->sbht", own_queries, fresh_keys, preferred_element_type=jnp.float32)
        * scale
    )
    causal = (
        jnp.arange(steps, dtype=jnp.int32)[:, None] >= jnp.arange(steps, dtype=jnp.int32)[None, :]
    )[:, None, None, :]
    fresh_scores = jnp.where(causal, fresh_scores, -1e30)
    top = jnp.maximum(own_top, jnp.max(fresh_scores, axis=-1))
    cache_factor = jnp.exp(own_top - top)
    fresh_weights = jnp.exp(fresh_scores - top[..., None])
    total = own_total * cache_factor + jnp.sum(fresh_weights, axis=-1)
    summed = own_sum * cache_factor[..., None] + jnp.einsum(
        "sbht,tbhd->sbhd", fresh_weights, fresh_values.astype(jnp.float32)
    )
    attn = (summed / total[..., None]).astype(jnp.bfloat16).reshape(rows, q_cols)
    blocks_in = o_cols // q_cols
    out_blocks = o_merged.reshape(q_cols, blocks_in, q_cols)
    partial_out = jnp.einsum(
        "snc,cjf->jnsf",
        lax.all_gather(attn.reshape(steps, seq_dev, q_cols), "dp", axis=1, tiled=True),
        out_blocks,
        preferred_element_type=jnp.float32,
    )
    dp_size = lax.axis_size("dp")
    tp_size = lax.axis_size("tp")
    arranged = partial_out.reshape(blocks_in * dp_size, seq_dev, steps, q_cols)
    spread_terms = jnp.zeros((tp_size * dp_size, seq_dev, steps, q_cols), jnp.float32)
    spread_terms = lax.dynamic_update_slice_in_dim(
        spread_terms, arranged, dp_index * blocks_in * dp_size, 0
    )
    own_rows = lax.psum_scatter(spread_terms, ("tp", "dp"), scatter_dimension=0, tiled=True)
    mixed = jnp.transpose(own_rows.reshape(seq_dev, steps, q_cols), (1, 0, 2)).astype(jnp.bfloat16)
    return mixed


def on_device(
    tokens, lengths, cache_keys, cache_values, q_weight, kv_weight, o_weight, adapters, layout
):
    t = lax.axis_index("tp")
    d = lax.axis_index("dp")
    steps, seq_dev, feat_dev = tokens.shape
    rows = steps * seq_dev
    span = cache_keys.shape[1]
    kv_cols = cache_keys.shape[2] // SIDE
    shards = layout.shape[0]
    numbers = jnp.arange(shards, dtype=jnp.int32)
    inverse = jnp.sum(jnp.where(layout[None, :] == numbers[:, None], numbers[None, :], 0), axis=1)
    row_d, across_d = block_places(inverse, d * SIDE, t, d)
    row_t, across_t = block_places(inverse, t * SIDE, t, d)
    y = lax.axis_index("groups")
    turn = t ^ d
    q_slots = jnp.concatenate([row_d, row_t, across_d, across_t, jnp.stack([y, turn])])
    o_slots = jnp.concatenate([row_t, row_d, across_t, across_d, jnp.stack([y, turn])])
    own = tokens.reshape(rows, feat_dev)
    rank = adapters.shape[1]
    halves = adapters.reshape(4, 2, rank // 2, adapters.shape[2])

    def shaped(*shape):
        return jax.ShapeDtypeStruct(shape, BF16)

    width = adapters.shape[2]
    slab = rows * feat_dev // width
    payload = first_call(y.reshape(1), halves, tokens, shaped(2 * rank + slab, width))
    held = [payload] + [along_tp(payload, k) for k in range(1, SIDE)]
    halves_far = across_dp(after(halves, payload), 2)

    ks = jnp.arange(SIDE, dtype=jnp.int32)
    froms = (t - (d ^ ks)) % SIDE
    spots = jnp.concatenate([(t - ks) % SIDE, lengths])
    cached = seq_dev * span
    cache_send = split_call(
        (t + ks) % SIDE,
        own,
        cache_keys.reshape(cached, -1),
        cache_values.reshape(cached, -1),
        kv_weight,
        shaped(2 * cached + 4 * rows, kv_cols),
    )

    *held, halves_far = lax.optimization_barrier((*held, halves_far))
    held = after(held, *cache_send, q_slots, o_slots, spots, froms)
    unit = (rank // 2, width)
    slab = slab // unit[0]
    others = 2 * (SIDE - 1)
    q_mine, o_mine, across, own_rows, near_rows = small_call(
        sort_kernel,
        froms,
        held,
        [shaped(n, *unit) for n in (others, others, others + 2 * slab, slab, slab)],
    )
    q_far = across_dp(across, 2)
    q_other = across_groups(q_mine)
    next_send, last_send = after([cache_send[1], cache_send[3]], q_mine)
    from_next, from_last = along_tp(next_send, 1), along_tp(last_send, 3)
    q_far, q_other, from_next, from_last = lax.optimization_barrier(
        (q_far, q_other, from_next, from_last)
    )
    middle_keys = along_tp(after(cache_send[2][:cached], q_far, q_other), 2)
    q_corners = corners_of(q_far, q_other)
    halves = halves.reshape(8, *unit)
    halves_far = halves_far.reshape(8, *unit)
    q_packed = pack([(halves, 0, 4), (halves_far, 0, 4), q_mine, q_far, q_other, near_rows])
    q_parts = with_sibling(q_packed, q_corners)
    o_mine = after(o_mine, *q_corners)
    o_far, o_other = across_dp(o_mine, 2), across_groups(o_mine)

    q_part = merge_call(
        merge_dot_kernel,
        q_slots,
        q_parts,
        pltpu.with_memory_space_constraint(q_weight, pltpu.HBM),
        [own_rows, q_far],
        jax.ShapeDtypeStruct((SIDE * rows, q_weight.shape[1]), F32),
        [4 * SIDE, SIDE, q_weight.shape[0] // BLOCK],
        rank,
        0,
    )
    q_part, middle_keys, middle_send, o_far, o_other = lax.optimization_barrier(
        (q_part, middle_keys, cache_send[2][cached:], o_far, o_other)
    )
    near = across_dp(jnp.concatenate([q_part[rows : 2 * rows], q_part[3 * rows :]]), 1)
    near, o_far, o_other = lax.optimization_barrier((near, o_far, o_other))
    middle_rest = along_tp(middle_send, 2)
    caches = [cache_send[0], from_next, from_last, middle_keys, middle_rest]
    q_near_sum = q_part[:rows] + near[:rows]
    q_far_sum = across_dp(q_part[2 * rows : 3 * rows] + near[rows:], 2)

    o_corners = corners_of(o_far, o_other)
    o_packed = pack([(halves, 4, 4), (halves_far, 4, 4), o_mine, o_far, o_other])
    o_parts = with_sibling(o_packed, o_corners)

    vmem_spec = pl.BlockSpec(memory_space=pltpu.VMEM)
    attn = pl.pallas_call(
        functools.partial(attention_kernel, seq_dev),
        out_shape=jax.ShapeDtypeStruct((rows, q_weight.shape[1]), BF16),
        in_specs=[pl.BlockSpec(memory_space=pltpu.SMEM)] + [vmem_spec] * 7,
        out_specs=vmem_spec,
        compiler_params=pltpu.CompilerParams(vmem_limit_bytes=8 * MIB),
    )(spots, q_near_sum, q_far_sum, *caches)

    o_merged = merge_call(
        merge_kernel,
        o_slots,
        o_parts,
        pltpu.with_memory_space_constraint(o_weight, pltpu.HBM),
        [],
        pltpu.VMEM(o_weight.shape, BF16),
        [4 * SIDE, o_weight.shape[0] // BLOCK],
        rank,
        16,
    )
    attn_rows = [attn] + [across_dp(attn, k) for k in range(1, SIDE)]
    width = o_weight.shape[1]
    first, rest = pl.pallas_call(
        out_kernel,
        out_shape=(
            jax.ShapeDtypeStruct((rows, width), F32),
            jax.ShapeDtypeStruct((SIDE - 1, rows, width), BF16),
        ),
        in_specs=[pl.BlockSpec(memory_space=pltpu.SMEM)] + [vmem_spec] * (SIDE + 1),
        out_specs=(vmem_spec, vmem_spec),
        scratch_shapes=[pltpu.VMEM((SIDE * rows, o_weight.shape[0]), BF16)],
        compiler_params=pltpu.CompilerParams(vmem_limit_bytes=16 * MIB),
    )(turn.reshape(1), *attn_rows, o_merged)
    mixed = to_holder(first, 0)
    for m in range(1, SIDE):
        mixed = mixed + to_holder(rest[m - 1], m).astype(F32)
    return mixed.astype(BF16).reshape(steps, seq_dev, width)


def solution(mesh):
    def fits(layout, cache_keys):
        sides = mesh.shape["tp"] == SIDE and mesh.shape["dp"] == SIDE and mesh.shape["groups"] == 2
        return sides and layout.shape[0] == SIDE * SIDE

    def run(tokens, lengths, cache_keys, cache_values, q_weight, kv_weight, o_weight, adapters, layout):
        body = on_device if fits(layout, cache_keys) else general
        return body(
            tokens, lengths, cache_keys, cache_values, q_weight, kv_weight, o_weight, adapters, layout
        )

    return jax.shard_map(
        run,
        mesh=mesh,
        in_specs=(
            P(None, ("groups", "dp"), "tp"),
            P(("groups", "dp")),
            P(("groups", "dp"), "tp", None),
            P(("groups", "dp"), "tp", None),
            P("dp", "tp"),
            P("tp", None),
            P("tp", "dp"),
            P(None, None, ("tp", "dp")),
            P(),
        ),
        out_specs=P(None, ("groups", "dp"), "tp"),
        check_vma=False,
    )
```

```python
import functools

import jax
import jax.numpy as jnp
from jax import lax
from jax.experimental import pallas as pl
from jax.experimental.pallas import tpu as pltpu
from jax.sharding import PartitionSpec as P

HD = 128
F32 = jnp.float32
BF16 = jnp.bfloat16
SIDE = 4
BLOCK = 256
MIB = 1 << 20


def after(x, *earlier):
    return lax.optimization_barrier((x, *earlier))[0]


def along_tp(x, k):
    return lax.ppermute(x, "tp", [(i, (i + k) % SIDE) for i in range(SIDE)])


def across_dp(x, k):
    return lax.ppermute(x, "dp", [(i, i ^ k) for i in range(SIDE)])


def across_groups(x):
    return lax.ppermute(x, "groups", [(0, 1), (1, 0)])


def to_holder(x, m):
    pairs = [(t * SIDE + d, d * SIDE + (t ^ m)) for t in range(SIDE) for d in range(SIDE)]
    return lax.ppermute(x, ("tp", "dp"), pairs)


def pack_kernel(spans, *refs):
    out_ref, at = refs[-1], 0
    for ref, (start, count) in zip(refs[:-1], spans):
        out_ref[at : at + count] = ref[start : start + count]
        at += count


def pack(parts):
    spec = pl.BlockSpec(memory_space=pltpu.VMEM)
    parts = [part if isinstance(part, tuple) else (part, 0, part.shape[0]) for part in parts]
    arrays = [array for array, _, _ in parts]
    spans = [(start, count) for _, start, count in parts]
    shape = (sum(count for _, count in spans), *arrays[0].shape[1:])
    return pl.pallas_call(
        functools.partial(pack_kernel, spans),
        out_shape=jax.ShapeDtypeStruct(shape, arrays[0].dtype),
        in_specs=[spec] * len(parts),
        out_specs=spec,
        compiler_params=pltpu.CompilerParams(vmem_limit_bytes=4 * MIB),
    )(*arrays)


def small_call(kernel, scalars, arrays, out_shape, vmem=8 * MIB):
    spec = pl.BlockSpec(memory_space=pltpu.VMEM)
    return pl.pallas_call(
        kernel,
        out_shape=out_shape,
        in_specs=[pl.BlockSpec(memory_space=pltpu.SMEM)] + [spec] * len(arrays),
        out_specs=jax.tree.map(lambda _: spec, out_shape),
        compiler_params=pltpu.CompilerParams(vmem_limit_bytes=vmem),
    )(scalars, *arrays)


def first_kernel(y_ref, adapters_ref, tokens_ref, out_ref, held_ref, sem):
    half = adapters_ref.shape[2]
    width = out_ref.shape[1]
    steps, seqs, depth = tokens_ref.shape
    rows = steps * seqs
    copies = [pltpu.make_async_copy(tokens_ref, held_ref, sem.at[4])]
    for f in range(4):
        copies.append(
            pltpu.make_async_copy(
                adapters_ref.at[f, y_ref[0]], out_ref.at[pl.ds(f * half, half)], sem.at[f]
            )
        )
    for copy in copies:
        copy.start()
    copies[0].wait()
    flat_rows = jnp.concatenate([held_ref[s].astype(F32) for s in range(steps)], axis=0)
    for j in range(depth // width):
        at = 4 * half + j * rows
        out_ref[at : at + rows] = flat_rows[:, j * width : (j + 1) * width].astype(BF16)
    for copy in copies[1:]:
        copy.wait()


def first_call(y, halves, tokens, out_shape):
    any_spec = pl.BlockSpec(memory_space=pl.ANY)
    return pl.pallas_call(
        first_kernel,
        out_shape=out_shape,
        in_specs=[pl.BlockSpec(memory_space=pltpu.SMEM), any_spec, any_spec],
        out_specs=pl.BlockSpec(memory_space=pltpu.VMEM),
        scratch_shapes=[pltpu.VMEM(tokens.shape, BF16), pltpu.SemaphoreType.DMA((5,))],
        compiler_params=pltpu.CompilerParams(vmem_limit_bytes=4 * MIB),
    )(
        y,
        pltpu.with_memory_space_constraint(halves, pltpu.HBM),
        pltpu.with_memory_space_constraint(tokens, pltpu.HBM),
    )


def sort_kernel(from_ref, *refs):
    held, (q_ref, o_ref, across_ref, *sends) = refs[:SIDE], refs[SIDE:]
    half = q_ref.shape[1]
    others = SIDE - 1
    for k in range(1, SIDE):
        for f in range(2):
            unit = held[k][f * half : (f + 1) * half]
            q_ref[f * others + k - 1] = unit
            across_ref[f * others + k - 1] = unit
            o_ref[f * others + k - 1] = held[k][(2 + f) * half : (3 + f) * half]
    slab = sends[0].shape[0]
    for k in range(SIDE):
        for j, ref in enumerate(held):

            @pl.when(from_ref[k] == j)
            def _(ref=ref, k=k):
                for u in range(slab):
                    unit = ref[(4 + u) * half : (5 + u) * half]
                    if k < 2:
                        sends[k][u] = unit
                    else:
                        across_ref[2 * others + (k - 2) * slab + u] = unit


def split_kernel(heads_ref, tokens_ref, keys_ref, values_ref, w_hbm, *refs):
    outs, (w_ref, kv_ref, sem) = refs[:SIDE], refs[SIDE:]
    row_parts = row_copies(w_hbm, w_ref, sem)
    for copy in row_parts:
        copy.start()
    cached = keys_ref.shape[0]
    rows, width = kv_ref.shape
    cols = outs[0].shape[1]
    places = [pl.multiple_of(heads_ref[k] * cols, cols) for k in range(SIDE)]
    for at, out in zip(places, outs):
        out[:cached] = keys_ref[:, pl.ds(at, cols)]
        out[cached : 2 * cached] = values_ref[:, pl.ds(at, cols)]
    for i in range(0, w_ref.shape[0], BLOCK):
        row_parts[i // BLOCK].wait()
        lanes = slice(i, i + BLOCK)
        term = jnp.dot(tokens_ref[:, lanes], w_ref[lanes, :], preferred_element_type=F32)
        if i == 0:
            kv_ref[...] = term
        else:
            kv_ref[...] += term
    for at, out in zip(places, outs):
        for part in range(2):
            term = kv_ref[:, pl.ds(pl.multiple_of(part * (width // 2) + at, cols), cols)]
            coarse = term.astype(BF16)
            row = 2 * cached + part * rows
            out[row : row + rows] = coarse
            out[row + 2 * rows : row + 3 * rows] = (term - coarse.astype(F32)).astype(BF16)


def split_call(heads, own, keys, values, weight, out_shape):
    spec = pl.BlockSpec(memory_space=pltpu.VMEM)
    return pl.pallas_call(
        split_kernel,
        out_shape=[out_shape] * SIDE,
        in_specs=[pl.BlockSpec(memory_space=pltpu.SMEM)]
        + [spec] * 3
        + [pl.BlockSpec(memory_space=pl.ANY)],
        out_specs=[spec] * SIDE,
        scratch_shapes=[
            pltpu.VMEM(weight.shape, BF16),
            pltpu.VMEM((own.shape[0], weight.shape[1]), F32),
            pltpu.SemaphoreType.DMA((weight.shape[0] // BLOCK,)),
        ],
        compiler_params=pltpu.CompilerParams(vmem_limit_bytes=16 * MIB),
        cost_estimate=pl.CostEstimate(
            flops=2 * own.size * weight.shape[1], bytes_accessed=4 * weight.size, transcendentals=0
        ),
    )(heads, own, keys, values, pltpu.with_memory_space_constraint(weight, pltpu.HBM))


def corners_of(mine_far, other):
    half = other.shape[0] // 2
    return [across_dp(other[:half], 2), across_groups(mine_far[half : 2 * half])]


def with_sibling(packed, corners):
    near = [packed, *corners]
    return near + [across_dp(x, 1) for x in near]


def block_places(inverse, first, t, d):
    source = lax.dynamic_slice_in_dim(inverse, first, SIDE, 0)
    return (t - source // SIDE) % SIDE, (source % SIDE) ^ d


def pick(slots_ref, parts, other_at, down_ref, up_ref, sem):
    y = slots_ref[4 * SIDE]
    half = down_ref.shape[0] // 2
    cols = down_ref.shape[1] // SIDE
    others = SIDE - 1

    def copy(n, source, h):
        dst = down_ref if n < SIDE else up_ref
        at = pl.multiple_of(h * half, half)
        lanes = pl.ds((n % SIDE) * cols, cols)
        return pltpu.make_async_copy(source, dst.at[pl.ds(at, half), lanes], sem.at[2 * n + h])

    for n in range(2 * SIDE):
        factor = n // SIDE
        row, across = slots_ref[n], slots_ref[2 * SIDE + n]
        far = across >> 1
        in_row = factor * others + row - 1
        at_mine = jnp.where(row == 0, far * 4 + factor * 2 + y, 8 + far * 2 * others + in_row)
        at_other = jnp.where(row == 0, far * 4 + factor * 2 + 1 - y, other_at + in_row)
        corner = (far == 1) & (row > 0)
        for side in range(2):
            packed, *corners = parts[side * 3 : side * 3 + 3]
            here = (across & 1) == side

            @pl.when(here)
            def _(packed=packed, at_mine=at_mine, n=n):
                copy(n, packed.at[at_mine], y).start()

            @pl.when(here & jnp.logical_not(corner))
            def _(packed=packed, at_other=at_other, n=n):
                copy(n, packed.at[at_other], 1 - y).start()

            @pl.when(here & corner)
            def _(source=corners[factor], row=row, n=n):
                copy(n, source.at[row - 1], 1 - y).start()

    for n in range(2 * SIDE):
        for h in range(2):
            copy(n, parts[0].at[0], h).wait()


def merged_rows(w, down_ref, up_ref, lanes):
    delta = lax.dot_general(
        down_ref[:, lanes], up_ref[...], (((0,), (0,)), ((), ())), preferred_element_type=F32
    )
    return (w.astype(F32) + delta).astype(BF16)


def row_copies(src, dst, sem):
    return [
        pltpu.make_async_copy(src.at[pl.ds(i, BLOCK)], dst.at[pl.ds(i, BLOCK)], sem.at[i // BLOCK])
        for i in range(0, src.shape[0], BLOCK)
    ]


def place_rows(turn, pieces, x_ref):
    rows = pieces[0].shape[0]
    for m, piece in enumerate(pieces):
        x_ref[pl.ds(pl.multiple_of((turn ^ m) * rows, rows), rows), :] = piece[...]


def merge_dot_kernel(slots_ref, *refs):
    parts = refs[:6]
    w_hbm, own_ref, across_ref, out_ref, down_ref, up_ref, w_ref, x_ref, tokens_ref = refs[6:15]
    sem, token_sem, row_sem = refs[15:]
    slab, half, width = own_ref.shape
    total = parts[3].shape[0]
    at = 2 * (SIDE - 1)
    sources = [
        own_ref,
        parts[3].at[pl.ds(total - slab, slab)],
        across_ref.at[pl.ds(at, slab)],
        parts[3].at[pl.ds(total - 2 * slab - at, slab)],
    ]
    copies = [
        pltpu.make_async_copy(source, tokens_ref.at[pl.ds(k * slab, slab)], token_sem.at[k])
        for k, source in enumerate(sources)
    ]
    row_parts = row_copies(w_hbm, w_ref, row_sem)
    for copy in copies + row_parts:
        copy.start()
    pick(slots_ref, parts, total - slab - at, down_ref, up_ref, sem)
    for copy in copies:
        copy.wait()
    rows = slab * half * width // x_ref.shape[1]
    for k in range(SIDE):
        for j in range(x_ref.shape[1] // width):
            u, row = divmod(j * rows, half)
            term = tokens_ref[k * slab + u, row : row + rows, :]
            x_ref[k * rows : (k + 1) * rows, j * width : (j + 1) * width] = term
    for i in range(0, w_ref.shape[0], BLOCK):
        row_parts[i // BLOCK].wait()
        lanes = slice(i, i + BLOCK)
        merged = merged_rows(w_ref[lanes, :], down_ref, up_ref, lanes)
        term = jnp.dot(x_ref[:, lanes], merged, preferred_element_type=F32)
        if i == 0:
            out_ref[...] = term
        else:
            out_ref[...] += term


def merge_kernel(slots_ref, *refs):
    w_ref, out_ref, down_ref, up_ref, sem, row_sem = refs[6:]
    copies = row_copies(w_ref, out_ref, row_sem)
    for copy in copies:
        copy.start()
    pick(slots_ref, refs[:6], refs[0].shape[0] - 2 * (SIDE - 1), down_ref, up_ref, sem)
    for i in range(0, w_ref.shape[0], BLOCK):
        copies[i // BLOCK].wait()
        lanes = slice(i, i + BLOCK)
        out_ref[lanes, :] = merged_rows(out_ref[lanes, :], down_ref, up_ref, lanes)


def merge_call(kernel, slots, parts, weight, pieces, out_shape, sems, rank, cost):
    depth, width = weight.shape
    piece_cols = parts[0].shape[-1]
    vmem_spec = pl.BlockSpec(memory_space=pltpu.VMEM)
    scratch = [pltpu.VMEM((rank, SIDE * piece_cols), BF16)] * 2
    if pieces:
        scratch.append(pltpu.VMEM(weight.shape, BF16))
        scratch.append(pltpu.VMEM((out_shape.shape[0], depth), BF16))
        slab, *unit = pieces[0].shape
        scratch.append(pltpu.VMEM((SIDE * slab, *unit), BF16))
    scratch += [pltpu.SemaphoreType.DMA((count,)) for count in sems]
    return pl.pallas_call(
        kernel,
        out_shape=out_shape,
        in_specs=[pl.BlockSpec(memory_space=pltpu.SMEM)]
        + [pl.BlockSpec(memory_space=pl.ANY)] * len(parts)
        + [pl.BlockSpec(memory_space=pl.ANY)]
        + [vmem_spec] * len(pieces),
        out_specs=vmem_spec,
        scratch_shapes=scratch,
        compiler_params=pltpu.CompilerParams(vmem_limit_bytes=16 * MIB),
        cost_estimate=pl.CostEstimate(flops=0, bytes_accessed=cost * MIB, transcendentals=0),
    )(slots, *parts, weight, *pieces)


def bias_kernel(seqs, spots_ref, bias_ref, fresh_ref):
    rows, cached = bias_ref.shape[1:]
    span = cached // seqs
    row_seq = lax.broadcasted_iota(jnp.int32, (rows, cached), 0) % seqs
    column = lax.broadcasted_iota(jnp.int32, (rows, cached), 1)
    for k in range(SIDE):
        valid = column < 0
        for b in range(seqs):
            left = jnp.clip(spots_ref[SIDE + b] - spots_ref[k] * span, 0, span)
            inside = (column >= b * span) & (column < b * span + left)
            valid |= inside & (row_seq == b)
        bias_ref[k] = jnp.where(valid, 0.0, -1e30)
    row = lax.broadcasted_iota(jnp.int32, (rows, rows), 0)
    earlier = lax.broadcasted_iota(jnp.int32, (rows, rows), 1)
    causal = (earlier // seqs <= row // seqs) & (earlier % seqs == row % seqs)
    fresh_ref[...] = jnp.where(causal, 0.0, -1e30)


def attention_kernel(bias_ref, fresh_ref, qa_ref, qb_ref, c0, c1, c3, keys_ref, rest_ref, out_ref):
    scale = HD ** (-0.5)
    rows = qa_ref.shape[0]
    kv_dev = c0.shape[1] // HD
    group = qa_ref.shape[1] // HD // kv_dev
    cached = bias_ref.shape[2]
    queries = (qa_ref[...] + qb_ref[...]).astype(BF16)

    def fresh_part(part):
        terms = []
        for c in (c0, c1, rest_ref, c3):
            at = c.shape[0] - 4 * rows + part * rows
            terms.append(c[at : at + rows].astype(F32))
            terms.append(c[at + 2 * rows : at + 3 * rows].astype(F32))
        return sum(terms).astype(BF16)

    fresh_keys, fresh_values = fresh_part(0), fresh_part(1)
    contract_last = (((1,), (1,)), ((), ()))

    def scores_of(q, keys, bias):
        s = lax.dot_general(q, keys, contract_last, preferred_element_type=F32) * scale
        s = s.reshape(group, rows, s.shape[1]) + bias[None]
        return s.reshape(group * rows, s.shape[2])

    def weighted(weights, values):
        coarse = weights.astype(BF16)
        rest = (weights - coarse.astype(F32)).astype(BF16)
        return jnp.dot(coarse, values, preferred_element_type=F32) + jnp.dot(
            rest, values, preferred_element_type=F32
        )

    for h in range(kv_dev):
        lanes = slice(h * HD, (h + 1) * HD)
        q = jnp.concatenate(
            [queries[:, (h * group + g) * HD : (h * group + g + 1) * HD] for g in range(group)], axis=0
        )
        scores = [scores_of(q, c[:cached, lanes], bias_ref[k]) for k, c in enumerate((c0, c1, keys_ref, c3))]
        scores.append(scores_of(q, fresh_keys[:, lanes], fresh_ref[...]))
        values = [c[cached : 2 * cached, lanes] for c in (c0, c1)]
        values += [rest_ref[:cached, lanes], c3[cached : 2 * cached, lanes]]
        values.append(fresh_values[:, lanes])
        top = functools.reduce(jnp.maximum, [jnp.max(s, axis=1, keepdims=True) for s in scores])
        weights = [jnp.exp(s - top) for s in scores]
        total = sum(jnp.sum(w, axis=1, keepdims=True) for w in weights)
        summed = sum(weighted(w, v) for w, v in zip(weights, values))
        attn = (summed / total).astype(BF16)
        for g in range(group):
            out_ref[:, (h * group + g) * HD : (h * group + g + 1) * HD] = attn[g * rows : (g + 1) * rows]


def out_kernel(turn_ref, a0, a1, a2, a3, w_ref, first_ref, rest_ref, x_ref):
    rows = a0.shape[0]
    place_rows(turn_ref[0], (a0, a1, a2, a3), x_ref)
    for j in range(0, w_ref.shape[1], 2 * BLOCK):
        lanes = slice(j, j + 2 * BLOCK)
        total = jnp.dot(x_ref[...], w_ref[:, lanes], preferred_element_type=F32)
        first_ref[:, lanes] = total[:rows]
        for m in range(1, SIDE):
            rest_ref[m - 1, :, lanes] = total[m * rows : (m + 1) * rows].astype(BF16)


def joined_2(array, axis, combine):
    everything = jax.tree.map(lambda part: lax.all_gather(part, axis), array)
    leading = jax.tree.map(lambda part: part[0], everything)

    def turn(k, so_far):
        return combine(so_far, jax.tree.map(lambda part: part[k], everything))

    return lax.fori_loop(1, lax.axis_size(axis), turn, leading)


def join_partials(first, second):
    top_a, total_a, summed_a = first
    top_b, total_b, summed_b = second
    top = jnp.maximum(top_a, top_b)
    factor_a = jnp.exp(top_a - top)
    factor_b = jnp.exp(top_b - top)
    return (
        top,
        total_a * factor_a + total_b * factor_b,
        summed_a * factor_a[..., None] + summed_b * factor_b[..., None],
    )


def pick_columns(stacked, inverse, factor, start, count):
    piece_cols = stacked.shape[3]
    block_ids = lax.dynamic_slice_in_dim(inverse, start // piece_cols, count // piece_cols, 0)
    chosen = jnp.take(stacked[factor], block_ids, axis=1)
    return chosen.reshape(stacked.shape[1], count)


def general(
    tokens, lengths, cache_keys, cache_values, q_weight, kv_weight, o_weight, adapters, layout
):
    tp_index = lax.axis_index("tp")
    dp_index = lax.axis_index("dp")
    steps, seq_dev, feat_dev = tokens.shape
    rank = adapters.shape[1]
    shards = layout.shape[0]
    rows = steps * seq_dev
    scale = HD ** (-0.5)
    gathered = lax.all_gather(adapters, ("tp", "dp"), axis=2, tiled=True)
    width = gathered.shape[2]
    piece_cols = width // shards
    stacked = gathered.reshape(4, rank, shards, piece_cols)
    block_numbers = jnp.arange(shards, dtype=jnp.int32)
    inverse = jnp.sum(
        jnp.where(layout[None, :] == block_numbers[:, None], block_numbers[None, :], 0), axis=1
    )
    kv_part = jnp.dot(tokens.reshape(rows, feat_dev), kv_weight, preferred_element_type=jnp.float32)
    new_kv = lax.psum(kv_part, "tp").astype(jnp.bfloat16)
    full_tokens = lax.all_gather(tokens, "tp", axis=2, tiled=True)
    q_rows = q_weight.shape[0]
    q_cols = q_weight.shape[1]
    o_cols = o_weight.shape[1]
    col_start = tp_index * q_cols
    q_down_part = pick_columns(stacked, inverse, 0, dp_index * q_rows, q_rows)
    q_up_part = pick_columns(stacked, inverse, 1, col_start, q_cols)
    o_down_part = pick_columns(stacked, inverse, 2, col_start, q_cols)
    o_up_part = pick_columns(stacked, inverse, 3, dp_index * o_cols, o_cols)
    q_merged = (
        q_weight.astype(jnp.float32)
        + jnp.einsum("rf,rc->fc", q_down_part, q_up_part, preferred_element_type=jnp.float32)
    ).astype(jnp.bfloat16)
    o_merged = (
        o_weight.astype(jnp.float32)
        + jnp.einsum("rf,rc->fc", o_down_part, o_up_part, preferred_element_type=jnp.float32)
    ).astype(jnp.bfloat16)
    flat_tokens = full_tokens.reshape(rows, width)
    q_total = jnp.dot(
        flat_tokens,
        lax.all_gather(q_merged, "dp", axis=0, tiled=True),
        preferred_element_type=jnp.float32,
    )
    queries = q_total.astype(jnp.bfloat16).reshape(steps, seq_dev, q_cols)
    all_queries = lax.all_gather(queries, "tp", axis=2, tiled=True)
    heads = all_queries.shape[2] // HD
    kv_heads = cache_keys.shape[2] // HD
    group = heads // kv_heads
    head_dev = q_cols // HD
    span = cache_keys.shape[1]
    grouped = all_queries.reshape(steps, seq_dev, kv_heads, group, HD)
    keys_local = cache_keys.reshape(seq_dev, span, kv_heads, HD)
    values_local = cache_values.reshape(seq_dev, span, kv_heads, HD)
    positions = tp_index * span + jnp.arange(span, dtype=jnp.int32)
    valid = (positions[None, :] < lengths[:, None])[None, :, None, None, :]
    scores = (
        jnp.einsum("sbkgd,bpkd->sbkgp", grouped, keys_local, preferred_element_type=jnp.float32)
        * scale
    )
    scores = jnp.where(valid, scores, -1e30)
    local_top = jnp.max(scores, axis=-1)
    weights = jnp.where(valid, jnp.exp(scores - local_top[..., None]), 0.0)
    local_total = jnp.sum(weights, axis=-1).reshape(steps, seq_dev, heads)
    local_sum = jnp.einsum("sbkgp,bpkd->sbkgd", weights, values_local.astype(jnp.float32)).reshape(
        steps, seq_dev, heads, HD
    )
    local_top = local_top.reshape(steps, seq_dev, heads)
    joined = joined_2((local_top, local_total, local_sum), "tp", join_partials)
    own_top = lax.dynamic_slice_in_dim(joined[0], tp_index * head_dev, head_dev, 2)
    own_total = lax.dynamic_slice_in_dim(joined[1], tp_index * head_dev, head_dev, 2)
    own_sum = lax.dynamic_slice_in_dim(joined[2], tp_index * head_dev, head_dev, 2)
    fresh = new_kv.reshape(steps, seq_dev, 2, kv_heads, HD)
    fresh_keys = lax.dynamic_slice_in_dim(
        jnp.repeat(fresh[:, :, 0], group, axis=2), tp_index * head_dev, head_dev, 2
    )
    fresh_values = lax.dynamic_slice_in_dim(
        jnp.repeat(fresh[:, :, 1], group, axis=2), tp_index * head_dev, head_dev, 2
    )
    own_queries = queries.reshape(steps, seq_dev, head_dev, HD)
    fresh_scores = (
        jnp.einsum("sbhd,tbhd->sbht", own_queries, fresh_keys, preferred_element_type=jnp.float32)
        * scale
    )
    causal = (
        jnp.arange(steps, dtype=jnp.int32)[:, None] >= jnp.arange(steps, dtype=jnp.int32)[None, :]
    )[:, None, None, :]
    fresh_scores = jnp.where(causal, fresh_scores, -1e30)
    top = jnp.maximum(own_top, jnp.max(fresh_scores, axis=-1))
    cache_factor = jnp.exp(own_top - top)
    fresh_weights = jnp.exp(fresh_scores - top[..., None])
    total = own_total * cache_factor + jnp.sum(fresh_weights, axis=-1)
    summed = own_sum * cache_factor[..., None] + jnp.einsum(
        "sbht,tbhd->sbhd", fresh_weights, fresh_values.astype(jnp.float32)
    )
    attn = (summed / total[..., None]).astype(jnp.bfloat16).reshape(rows, q_cols)
    blocks_in = o_cols // q_cols
    out_blocks = o_merged.reshape(q_cols, blocks_in, q_cols)
    partial_out = jnp.einsum(
        "snc,cjf->jnsf",
        lax.all_gather(attn.reshape(steps, seq_dev, q_cols), "dp", axis=1, tiled=True),
        out_blocks,
        preferred_element_type=jnp.float32,
    )
    dp_size = lax.axis_size("dp")
    tp_size = lax.axis_size("tp")
    arranged = partial_out.reshape(blocks_in * dp_size, seq_dev, steps, q_cols)
    spread_terms = jnp.zeros((tp_size * dp_size, seq_dev, steps, q_cols), jnp.float32)
    spread_terms = lax.dynamic_update_slice_in_dim(
        spread_terms, arranged, dp_index * blocks_in * dp_size, 0
    )
    own_rows = lax.psum_scatter(spread_terms, ("tp", "dp"), scatter_dimension=0, tiled=True)
    mixed = jnp.transpose(own_rows.reshape(seq_dev, steps, q_cols), (1, 0, 2)).astype(jnp.bfloat16)
    return mixed


def on_device(
    tokens, lengths, cache_keys, cache_values, q_weight, kv_weight, o_weight, adapters, layout
):
    t = lax.axis_index("tp")
    d = lax.axis_index("dp")
    steps, seq_dev, feat_dev = tokens.shape
    rows = steps * seq_dev
    span = cache_keys.shape[1]
    kv_cols = cache_keys.shape[2] // SIDE
    shards = layout.shape[0]
    numbers = jnp.arange(shards, dtype=jnp.int32)
    inverse = jnp.sum(jnp.where(layout[None, :] == numbers[:, None], numbers[None, :], 0), axis=1)
    row_d, across_d = block_places(inverse, d * SIDE, t, d)
    row_t, across_t = block_places(inverse, t * SIDE, t, d)
    y = lax.axis_index("groups")
    turn = t ^ d
    q_slots = jnp.concatenate([row_d, row_t, across_d, across_t, jnp.stack([y, turn])])
    o_slots = jnp.concatenate([row_t, row_d, across_t, across_d, jnp.stack([y, turn])])
    own = tokens.reshape(rows, feat_dev)
    rank = adapters.shape[1]
    halves = adapters.reshape(4, 2, rank // 2, adapters.shape[2])

    def shaped(*shape):
        return jax.ShapeDtypeStruct(shape, BF16)

    width = adapters.shape[2]
    slab = rows * feat_dev // width
    payload = first_call(y.reshape(1), halves, tokens, shaped(2 * rank + slab, width))
    held = [payload] + [along_tp(payload, k) for k in range(1, SIDE)]
    halves_far = across_dp(after(halves, payload), 2)

    ks = jnp.arange(SIDE, dtype=jnp.int32)
    froms = (t - (d ^ ks)) % SIDE
    spots = jnp.concatenate([(t - ks) % SIDE, lengths])
    cached = seq_dev * span
    cache_send = split_call(
        (t + ks) % SIDE,
        own,
        cache_keys.reshape(cached, -1),
        cache_values.reshape(cached, -1),
        kv_weight,
        shaped(2 * cached + 4 * rows, kv_cols),
    )

    bias, fresh_bias = small_call(
        functools.partial(bias_kernel, seq_dev),
        spots,
        [],
        [
            jax.ShapeDtypeStruct((SIDE, rows, seq_dev * span), F32),
            jax.ShapeDtypeStruct((rows, rows), F32),
        ],
    )
    *held, halves_far, bias, fresh_bias = lax.optimization_barrier(
        (*held, halves_far, bias, fresh_bias)
    )
    held = after(held, *cache_send, q_slots, o_slots, spots, froms)
    unit = (rank // 2, width)
    slab = slab // unit[0]
    others = 2 * (SIDE - 1)
    q_mine, o_mine, across, own_rows, near_rows = small_call(
        sort_kernel,
        froms,
        held,
        [shaped(n, *unit) for n in (others, others, others + 2 * slab, slab, slab)],
    )
    q_far = across_dp(across, 2)
    q_other = across_groups(q_mine)
    next_send, last_send = after([cache_send[1], cache_send[3]], q_mine)
    from_next, from_last = along_tp(next_send, 1), along_tp(last_send, 3)
    q_far, q_other, from_next, from_last = lax.optimization_barrier(
        (q_far, q_other, from_next, from_last)
    )
    middle_keys = along_tp(after(cache_send[2][:cached], q_far, q_other), 2)
    q_corners = corners_of(q_far, q_other)
    halves = halves.reshape(8, *unit)
    halves_far = halves_far.reshape(8, *unit)
    q_packed = pack([(halves, 0, 4), (halves_far, 0, 4), q_mine, q_far, q_other, near_rows])
    q_parts = with_sibling(q_packed, q_corners)
    o_mine = after(o_mine, *q_corners)
    o_far, o_other = across_dp(o_mine, 2), across_groups(o_mine)

    q_part = merge_call(
        merge_dot_kernel,
        q_slots,
        q_parts,
        pltpu.with_memory_space_constraint(q_weight, pltpu.HBM),
        [own_rows, q_far],
        jax.ShapeDtypeStruct((SIDE * rows, q_weight.shape[1]), F32),
        [4 * SIDE, SIDE, q_weight.shape[0] // BLOCK],
        rank,
        0,
    )
    q_part, middle_keys, middle_send, o_far, o_other = lax.optimization_barrier(
        (q_part, middle_keys, cache_send[2][cached:], o_far, o_other)
    )
    near = across_dp(jnp.concatenate([q_part[rows : 2 * rows], q_part[3 * rows :]]), 1)
    near, o_far, o_other = lax.optimization_barrier((near, o_far, o_other))
    middle_rest = along_tp(middle_send, 2)
    caches = [cache_send[0], from_next, from_last, middle_keys, middle_rest]
    q_near_sum = q_part[:rows] + near[:rows]
    q_far_sum = across_dp(q_part[2 * rows : 3 * rows] + near[rows:], 2)

    o_corners = corners_of(o_far, o_other)
    o_packed = pack([(halves, 4, 4), (halves_far, 4, 4), o_mine, o_far, o_other])
    o_parts = with_sibling(o_packed, o_corners)

    vmem_spec = pl.BlockSpec(memory_space=pltpu.VMEM)
    attn = pl.pallas_call(
        attention_kernel,
        out_shape=jax.ShapeDtypeStruct((rows, q_weight.shape[1]), BF16),
        in_specs=[vmem_spec] * 9,
        out_specs=vmem_spec,
        compiler_params=pltpu.CompilerParams(vmem_limit_bytes=8 * MIB),
    )(bias, fresh_bias, q_near_sum, q_far_sum, *caches)

    o_merged = merge_call(
        merge_kernel,
        o_slots,
        o_parts,
        pltpu.with_memory_space_constraint(o_weight, pltpu.HBM),
        [],
        pltpu.VMEM(o_weight.shape, BF16),
        [4 * SIDE, o_weight.shape[0] // BLOCK],
        rank,
        16,
    )
    attn_rows = [attn] + [across_dp(attn, k) for k in range(1, SIDE)]
    width = o_weight.shape[1]
    first, rest = pl.pallas_call(
        out_kernel,
        out_shape=(
            jax.ShapeDtypeStruct((rows, width), F32),
            jax.ShapeDtypeStruct((SIDE - 1, rows, width), BF16),
        ),
        in_specs=[pl.BlockSpec(memory_space=pltpu.SMEM)] + [vmem_spec] * (SIDE + 1),
        out_specs=(vmem_spec, vmem_spec),
        scratch_shapes=[pltpu.VMEM((SIDE * rows, o_weight.shape[0]), BF16)],
        compiler_params=pltpu.CompilerParams(vmem_limit_bytes=16 * MIB),
    )(turn.reshape(1), *attn_rows, o_merged)
    mixed = to_holder(first, 0)
    for m in range(1, SIDE):
        mixed = mixed + to_holder(rest[m - 1], m).astype(F32)
    return mixed.astype(BF16).reshape(steps, seq_dev, width)


def solution(mesh):
    def fits(layout, cache_keys):
        sides = mesh.shape["tp"] == SIDE and mesh.shape["dp"] == SIDE and mesh.shape["groups"] == 2
        return sides and layout.shape[0] == SIDE * SIDE

    def run(tokens, lengths, cache_keys, cache_values, q_weight, kv_weight, o_weight, adapters, layout):
        body = on_device if fits(layout, cache_keys) else general
        return body(
            tokens, lengths, cache_keys, cache_values, q_weight, kv_weight, o_weight, adapters, layout
        )

    return jax.shard_map(
        run,
        mesh=mesh,
        in_specs=(
            P(None, ("groups", "dp"), "tp"),
            P(("groups", "dp")),
            P(("groups", "dp"), "tp", None),
            P(("groups", "dp"), "tp", None),
            P("dp", "tp"),
            P("tp", None),
            P("tp", "dp"),
            P(None, None, ("tp", "dp")),
            P(),
        ),
        out_specs=P(None, ("groups", "dp"), "tp"),
        check_vma=False,
    )
```
